128 devices in a mesh: dp: 16 (over y, z), tensor: 8 (over x, core).
Axes of the slice: x: 4, y: 4, z: 4, core: 2. Of those that a mesh axis runs over, the one named last changes fastest.
Arguments:
- hidden_in: bfloat16 [16384, 2560], P('dp'), may hold values from -6 to 6
- ln_gain: float32 [2560], replicated, may hold values from 0.5 to 1.5
- attn_probs: bfloat16 [32, 24, 512, 512], P('dp', 'tensor'), may hold values from 9.727478e-05 to 0.009765625
- w_value: bfloat16 [2560, 3072], P(None, 'tensor'), may hold values from -0.5 to 0.5
- w_out: bfloat16 [3072, 2560], P('tensor'), may hold values from -0.109375 to 0.109375
- out_grad: bfloat16 [16384, 2560], P('dp'), may hold values from -6 to 6
- err_out: float32 [16, 3072, 2560], P('dp', 'tensor'), may hold values from -6 to 6
- err_value: float32 [16, 3072, 2560], P('dp', 'tensor'), may hold values from -6 to 6
- factor_codes: int32 [2], replicated, may hold values from 0 to 999999
Outputs:
- in_grad: bfloat16 [16384, 2560], P(('dp', 'tensor'))
- gain_grad: float32 [2560], replicated
- new_err_out: float32 [16, 3072, 2560], P('dp', 'tensor')
- new_err_value: float32 [16, 3072, 2560], P('dp', 'tensor')
- left_out: float32 [3072, 32], P('tensor')
- left_value: float32 [3072, 32], P('tensor')
- right_out: float32 [2560, 32], P('tensor')
- right_value: float32 [2560, 32], P('tensor')
The draws below stay inside these ranges and needn't reach their ends.
All inputs are finite; a program needn't handle non-finite values.
Results may differ from the reference program's by a relative error of at most 0.022.
Values may be sent and summed in bfloat16 or wider, within the bound.
No kernel may reach another device: no remote copies, remote signals or barrier semaphores. Data moves between devices by JAX's collectives and lax.ppermute only.
A program may use at most 192 MiB of HBM per device.

```python
import math
import jax
import jax.numpy as jnp
from jax import lax

D = 2560
HEADS = 24
HEAD_DIM = 128
RANK = 32
LEN = 512
SEQ_DEV = 2
HH = 3072
TOK_DEV = 1024
SEQS = 32
TOKENS = 16384
N_DP = 16
N_TENSOR = 8


def levels(key, shape, split, least, high):
    def one(dim, parts):
        heights = jax.random.uniform(jax.random.fold_in(jax.random.fold_in(key, 6), dim), (parts,), jnp.float32, least / len(split), high / len(split))
        return jnp.repeat(jnp.exp(heights), shape[dim] // parts).reshape((-1,) + (1,) * (len(shape) - dim - 1))

    loudness = one(*split[0])
    for cut in split[1:]:
        loudness = loudness * one(*cut)
    return loudness


def gaussian(own_key, shape, spread, most, split=(), dtype=jnp.bfloat16):
    values = spread * jax.random.normal(own_key, shape, jnp.float32)
    if split:
        values = values * levels(own_key, shape, split, -0.22, 0.18)
    return jnp.clip(values, -most, most).astype(dtype)


def setup_inputs(seed: int = 0) -> dict:
    arg_keys = jax.random.split(jax.random.key(seed), 10)
    return {
        "hidden_in": gaussian(arg_keys[0], (TOKENS, D), 1.0, 6.0, ((0, 16),)),
        "ln_gain": jnp.clip(1.0 + 0.1 * jax.random.normal(arg_keys[1], (D,), jnp.float32), 0.5, 1.5),
        "attn_probs": jnp.clip(jnp.exp(math.log(0.009765625) - 4.609084 * jax.random.uniform(arg_keys[2], (SEQS, HEADS, LEN, LEN), jnp.float32) ** levels(arg_keys[2], (SEQS, HEADS, LEN, LEN), ((0, 16), (1, 8)), -0.2, 0.2)), 9.72747802734375e-05, 0.009765625).astype(jnp.bfloat16),
        "w_value": gaussian(arg_keys[3], (D, HH), (D // 16) ** -0.5, 0.5, ((1, 8),)),
        "w_out": gaussian(arg_keys[4], (HH, D), HH ** -0.5, 0.109375, ((0, 8),)),
        "out_grad": gaussian(arg_keys[5], (TOKENS, D), 1.0, 6.0, ((0, 16),)),
        "err_out": gaussian(arg_keys[6], (N_DP, HH, D), 1.0, 6.0, ((0, 16), (1, 8)), jnp.float32),
        "err_value": gaussian(arg_keys[7], (N_DP, HH, D), 1.0, 6.0, ((0, 16), (1, 8)), jnp.float32),
        "factor_codes": jax.random.randint(arg_keys[8], (2,), 0, 1000000).astype(jnp.int32),
    }


def layer_stats(hidden, gain):
    widened = hidden.astype(jnp.float32)
    row_mean = lax.optimization_barrier(jnp.mean(widened, axis=-1, keepdims=True))
    centred = widened - row_mean
    inv_std = lax.rsqrt(lax.optimization_barrier(jnp.mean(centred * centred, axis=-1, keepdims=True)) + 1e-05)
    standard = centred * inv_std
    return (standard, inv_std, (standard * gain).astype(jnp.bfloat16))

def norm_back(branch_grad, standard, inv_std, gain):
    scaled = branch_grad * gain
    first_mean = lax.optimization_barrier(jnp.mean(scaled, axis=-1, keepdims=True))
    second_mean = lax.optimization_barrier(jnp.mean(scaled * standard, axis=-1, keepdims=True))
    result = inv_std * (scaled - first_mean - standard * second_mean)
    return (result.astype(jnp.bfloat16), lax.optimization_barrier(jnp.sum(branch_grad * standard, axis=0)))

def make_start(code):
    row_ids = lax.broadcasted_iota(jnp.int32, (D, RANK), 0)
    col_ids = lax.broadcasted_iota(jnp.int32, (D, RANK), 1)
    hashed = row_ids * 40503 + col_ids * 1531 + code.astype(jnp.int32) * 7919
    hashed = jnp.bitwise_xor(hashed, jnp.right_shift(hashed, 15)) * 668265261
    hashed = jnp.bitwise_xor(hashed, jnp.right_shift(hashed, 15)) * 374761393
    hashed = jnp.bitwise_xor(hashed, jnp.right_shift(hashed, 13))
    level = jnp.bitwise_and(hashed, 8388607).astype(jnp.float32)
    return ((level + 0.5) / 8388608.0 - 0.5) * math.sqrt(12.0)

def compress(grads, errors, code):
    mats = grads + errors
    start = make_start(code)
    left = jnp.einsum('whd,dr->hr', mats, start, precision=lax.Precision.HIGHEST) / N_DP
    gram = jnp.dot(left.T, left, precision=lax.Precision.HIGHEST)
    factor = jnp.linalg.cholesky(gram)
    ortho = lax.linalg.triangular_solve(factor, left, left_side=False, lower=True, transpose_a=True)
    right = jnp.einsum('whd,hr->dr', mats, ortho, precision=lax.Precision.HIGHEST) / N_DP
    fresh = mats - jnp.dot(ortho, right.T, precision=lax.Precision.HIGHEST)[None]
    return (fresh, ortho * math.sqrt(HEADS * HEAD_DIM), right)

def reference(hidden_in, ln_gain, attn_probs, w_value, w_out, out_grad, err_out, err_value, factor_codes):
    inner = HEADS * HEAD_DIM
    block_cols = inner // N_TENSOR

    def worker(pieces):
        hidden, probs, grad_y = pieces
        standard, inv_std, normed = layer_stats(hidden, ln_gain)
        values = jnp.dot(normed.astype(jnp.float32), w_value.astype(jnp.float32), preferred_element_type=jnp.float32).astype(jnp.bfloat16)
        shaped = values.reshape(SEQ_DEV, LEN, HEADS, HEAD_DIM).astype(jnp.float32)
        weights = probs.astype(jnp.float32)
        mixed = jnp.einsum('shqk,skhd->sqhd', weights, shaped).astype(jnp.bfloat16).reshape(TOK_DEV, inner)
        grad_outw = jnp.dot(mixed.T.astype(jnp.float32), grad_y.astype(jnp.float32), preferred_element_type=jnp.float32)
        d_mixed = jnp.dot(grad_y.astype(jnp.float32), w_out.T.astype(jnp.float32), preferred_element_type=jnp.float32).astype(jnp.bfloat16)
        d_shaped = d_mixed.reshape(SEQ_DEV, LEN, HEADS, HEAD_DIM).astype(jnp.float32)
        d_values = jnp.einsum('shqk,sqhd->skhd', weights, d_shaped).astype(jnp.bfloat16).reshape(TOK_DEV, inner)
        grad_valuew = jnp.dot(d_values.T.astype(jnp.float32), normed.astype(jnp.float32), preferred_element_type=jnp.float32)
        branch_grad = jnp.zeros((TOK_DEV, D), jnp.float32)
        for shard in range(N_TENSOR):
            lower = shard * block_cols
            upper = lower + block_cols
            product = jnp.dot(d_values[:, lower:upper].astype(jnp.float32), w_value[:, lower:upper].T.astype(jnp.float32), preferred_element_type=jnp.float32)
            branch_grad = branch_grad + lax.optimization_barrier(product.astype(jnp.bfloat16)).astype(jnp.float32)
        result, gain_part = norm_back(branch_grad, standard, inv_std, ln_gain)
        return (grad_outw, grad_valuew, result, gain_part)
    stacked = (hidden_in.reshape(N_DP, TOK_DEV, D), attn_probs.reshape(N_DP, SEQ_DEV, HEADS, LEN, LEN), out_grad.reshape(N_DP, TOK_DEV, D))
    grads_out, grads_value, results, gain_parts = lax.map(worker, stacked)
    in_grad = results.reshape(N_DP * TOK_DEV, D)
    gain_grad = lax.optimization_barrier(jnp.sum(gain_parts, axis=0))
    fresh_out, left_out, right_out = compress(grads_out, err_out, factor_codes[0])
    fresh_value, left_value, right_value = compress(grads_value, err_value, factor_codes[1])
    return (in_grad, gain_grad, fresh_out, fresh_value, left_out, left_value, right_out, right_value)
```

```python
import math

import jax
import jax.numpy as jnp
from jax import lax
from jax.experimental import pallas as pl
from jax.experimental.pallas import tpu as pltpu
from jax.sharding import PartitionSpec as P

D = 2560
RANK = 32
HEADS = 24
HEAD_DIM = 128
LEN = 512
CROPS = 2
HEADS_DEV = 3
TOK = CROPS * LEN
COLS = HEADS_DEV * HEAD_DIM
HH = HEADS * HEAD_DIM
TAIL = 128
WIDE = D + TAIL
TILE = 512
STEPS = D // TILE
WORKERS = 16
F32 = jnp.float32
BF16 = jnp.bfloat16
ANY = pl.BlockSpec(memory_space=pl.ANY)
SMEM = pl.BlockSpec(memory_space=pltpu.SMEM)


def dot(a, b, dims=((1,), (0,))):
    return lax.dot_general(a, b, (dims, ((), ())), preferred_element_type=F32)


def split2(a):
    high = a.astype(BF16)
    return high, (a - high.astype(F32)).astype(BF16)


def dot_split(a, b, dims=((1,), (0,))):
    a_high, a_low = split2(a)
    b_high, b_low = split2(b)
    return dot(a_high, b_high, dims) + (dot(a_low, b_high, dims) + dot(a_high, b_low, dims))


def lane_parts(value, group):
    high = value.astype(BF16).astype(F32)
    rest = value - high
    middle = rest.astype(BF16).astype(F32)
    low = rest - middle
    zero = jnp.zeros_like(value)
    return jnp.where(
        group == 0, high, jnp.where(group == 1, middle, jnp.where(group == 2, low, zero))
    ).astype(BF16)


def start_rows(code, first, rows):
    row_ids = lax.broadcasted_iota(jnp.int32, (rows, 128), 0) + first
    lane = lax.broadcasted_iota(jnp.int32, (rows, 128), 1)
    hashed = row_ids * 40503 + jnp.bitwise_and(lane, RANK - 1) * 1531 + code * 7919
    hashed = jnp.bitwise_xor(hashed, jnp.right_shift(hashed, 15)) * 668265261
    hashed = jnp.bitwise_xor(hashed, jnp.right_shift(hashed, 15)) * 374761393
    hashed = jnp.bitwise_xor(hashed, jnp.right_shift(hashed, 13))
    level = jnp.bitwise_and(hashed, 8388607).astype(F32)
    start = ((level + 0.5) / 8388608.0 - 0.5) * math.sqrt(12.0)
    return lane_parts(start, jnp.right_shift(lane, 5))


def all_groups(value):
    return (value + pltpu.roll(value, 64, 1)) + (pltpu.roll(value, 32, 1) + pltpu.roll(value, 96, 1))


def front_kernel(
    codes, gain, hidden, probs, w_value, w_out, out_grad, err_out, err_value,
    normed_out, mixed_t_out, d_values_t_out, left_out,
    hidden_v, probs_v, wv_ext, w_out_v, wo_ext, grad_v, err_out_v, err_value_v,
    normed_v, values_v, d_mixed_v, y_out, y_value, sems, out_sems,
):
    copies = [
        pltpu.make_async_copy(source, target, sems.at[index])
        for index, (source, target) in enumerate(
            (
                (w_out, w_out_v),
                (out_grad, grad_v),
                (hidden, hidden_v),
                (w_value, wv_ext.at[:, pl.ds(0, COLS)]),
                (probs, probs_v),
                (err_out.at[0], err_out_v),
                (err_value.at[0], err_value_v),
            )
        )
    ]
    for copy in copies:
        copy.start()

    @pl.loop(0, D // 128)
    def _(step):
        rows = pl.ds(pl.multiple_of(step * 128, 128), 128)
        wo_ext[rows, pl.ds(COLS, 128)] = start_rows(codes[0], step * 128, 128)
        wv_ext[rows, pl.ds(COLS, 128)] = start_rows(codes[1], step * 128, 128)

    copies[0].wait()

    @pl.loop(0, D // 256)
    def _(step):
        span = pl.ds(pl.multiple_of(step * 256, 256), 256)
        wo_ext[span, pl.ds(0, COLS)] = w_out_v[:, span].T

    copies[1].wait()

    @pl.loop(0, TOK // 256)
    def _(step):
        rows = pl.ds(pl.multiple_of(step * 256, 256), 256)
        product = dot(grad_v[rows, :], wo_ext[...])
        d_mixed_v[rows, :] = product[:, :COLS].astype(BF16)
        y_out[rows, :] = product[:, COLS:]

    copies[2].wait()

    def norm_rows(step, carry):
        rows = pl.ds(pl.multiple_of(step * 32, 32), 32)
        total = jnp.zeros((32, 128), F32)
        for part in range(D // 128):
            total = total + hidden_v[rows, pl.ds(part * 128, 128)].astype(F32)
        mean = jnp.sum(total, axis=1, keepdims=True) * (1.0 / D)
        total = jnp.zeros((32, 128), F32)
        for part in range(D // 128):
            centred = hidden_v[rows, pl.ds(part * 128, 128)].astype(F32) - mean
            total = total + centred * centred
        inv_std = lax.rsqrt(jnp.sum(total, axis=1, keepdims=True) * (1.0 / D) + 1e-05)
        for part in range(D // 128):
            lanes = pl.ds(part * 128, 128)
            centred = hidden_v[rows, lanes].astype(F32) - mean
            normed_v[rows, lanes] = (centred * inv_std * gain[:, lanes]).astype(BF16)
        return carry

    lax.fori_loop(0, TOK // 32, norm_rows, 0, unroll=4)
    normed_copy = pltpu.make_async_copy(normed_v, normed_out, out_sems.at[0])
    normed_copy.start()
    copies[3].wait()

    @pl.loop(0, TOK // 256)
    def _(step):
        rows = pl.ds(pl.multiple_of(step * 256, 256), 256)
        product = dot(normed_v[rows, :], wv_ext[...])
        values_v[rows, :] = product[:, :COLS].astype(BF16)
        y_value[rows, :] = product[:, COLS:]

    copies[4].wait()
    for crop in range(CROPS):
        rows = pl.ds(crop * LEN, LEN)
        for head in range(HEADS_DEV):
            cols = pl.ds(head * HEAD_DIM, HEAD_DIM)
            weights = probs_v[crop, head]
            mixed = dot(weights, values_v[rows, cols]).astype(BF16)
            mixed_t_out[cols, rows] = mixed.T
            d_mixed_t = d_mixed_v[rows, cols].T
            d_values_t_out[cols, rows] = dot(d_mixed_t, weights).astype(BF16)

    group = jnp.right_shift(lax.broadcasted_iota(jnp.int32, (TOK, 128), 1), 5)
    sides = (
        (copies[5], err_out_v, wo_ext, y_out, mixed_t_out),
        (copies[6], err_value_v, wv_ext, y_value, d_values_t_out),
    )
    for index, (copy, err_v, ext, y_ref, acts_t) in enumerate(sides):
        copy.wait()
        y_parts = lane_parts(all_groups(y_ref[...]), group)
        err_high, err_low = split2(err_v[...])
        start = ext[:, pl.ds(COLS, 128)]
        product = dot(acts_t[...], y_parts) + (dot(err_high, start) + dot(err_low, start))
        turned = product.T
        left_out[pl.ds(index * RANK, RANK), :] = (
            turned[0:32] + (turned[32:64] + turned[64:96])
        ).astype(BF16)
    normed_copy.wait()


def front(codes, gain, hidden, probs, w_value, w_out, out_grad, err_out, err_value):
    vmem = pl.BlockSpec(memory_space=pltpu.VMEM)
    return pl.pallas_call(
        front_kernel,
        name="front",
        out_shape=(
            jax.ShapeDtypeStruct((TOK, D), BF16),
            jax.ShapeDtypeStruct((COLS, TOK), BF16),
            jax.ShapeDtypeStruct((COLS, TOK), BF16),
            jax.ShapeDtypeStruct((2 * RANK, COLS), BF16),
        ),
        in_specs=[SMEM, vmem] + [ANY] * 7,
        out_specs=(ANY, vmem, vmem, vmem),
        scratch_shapes=[
            pltpu.VMEM((TOK, D), BF16),
            pltpu.VMEM((CROPS, HEADS_DEV, LEN, LEN), BF16),
            pltpu.VMEM((D, COLS + 128), BF16),
            pltpu.VMEM((COLS, D), BF16),
            pltpu.VMEM((D, COLS + 128), BF16),
            pltpu.VMEM((TOK, D), BF16),
            pltpu.VMEM((COLS, D), F32),
            pltpu.VMEM((COLS, D), F32),
            pltpu.VMEM((TOK, D), BF16),
            pltpu.VMEM((TOK, COLS), BF16),
            pltpu.VMEM((TOK, COLS), BF16),
            pltpu.VMEM((TOK, 128), F32),
            pltpu.VMEM((TOK, 128), F32),
            pltpu.SemaphoreType.DMA((7,)),
            pltpu.SemaphoreType.DMA((1,)),
        ],
        compiler_params=pltpu.CompilerParams(vmem_limit_bytes=56 * 2**20),
        cost_estimate=pl.CostEstimate(
            flops=11 * 10**9, bytes_accessed=32 * 10**6, transcendentals=0
        ),
    )(codes, gain, hidden, probs, w_value, w_out, out_grad, err_out, err_value)


def branch_kernel(place, d_values_t, w_value, normed, gain, own, other, gain_part, d_values):
    @pl.when(pl.program_id(0) == 0)
    def _():
        for block in range(TOK // 256):
            rows = pl.ds(block * 256, 256)
            d_values[rows, :] = d_values_t[:, rows].T

    product = dot(d_values[...], w_value[...], ((1,), (1,)))
    gain_part[...] = (
        jnp.sum(product * normed[...].astype(F32), axis=0, keepdims=True) / gain[...]
    )
    rounded = product.astype(BF16)
    chip, core = place[0], place[1]
    for block in range(8):
        slot = lax.rem(block // 2 - chip + 4, 4)
        part = rounded[block * 128 : (block + 1) * 128]

        @pl.when(core == block % 2)
        def _():
            own[slot] = part

        @pl.when(core != block % 2)
        def _():
            other[slot] = part


def branch(place, d_values_t, w_value, normed, gain):
    quarter = pl.BlockSpec((4, 128, TILE), lambda n: (0, 0, n))
    return pl.pallas_call(
        branch_kernel,
        name="branch",
        grid=(STEPS,),
        out_shape=(
            jax.ShapeDtypeStruct((4, 128, D), BF16),
            jax.ShapeDtypeStruct((4, 128, D), BF16),
            jax.ShapeDtypeStruct((1, D), F32),
        ),
        in_specs=[
            SMEM,
            pl.BlockSpec((COLS, TOK), lambda n: (0, 0)),
            pl.BlockSpec((TILE, COLS), lambda n: (n, 0)),
            pl.BlockSpec((TOK, TILE), lambda n: (0, n)),
            pl.BlockSpec((1, TILE), lambda n: (0, n)),
        ],
        out_specs=(quarter, quarter, pl.BlockSpec((1, TILE), lambda n: (0, n))),
        scratch_shapes=[pltpu.VMEM((TOK, COLS), BF16)],
        compiler_params=pltpu.CompilerParams(vmem_limit_bytes=40 * 2**20),
        cost_estimate=pl.CostEstimate(
            flops=2 * 10**9, bytes_accessed=13 * 10**6, transcendentals=0
        ),
    )(place, d_values_t, w_value, normed, gain)


def mats_kernel(acts_t, other_side, err, mats):
    mats[...] = dot(acts_t[...], other_side[...]) + err[0]


def mats_of(acts_t, other_side, err, name):
    return pl.pallas_call(
        mats_kernel,
        name=name,
        grid=(STEPS,),
        out_shape=jax.ShapeDtypeStruct((COLS, D), F32),
        in_specs=[
            pl.BlockSpec((COLS, TOK), lambda n: (0, 0)),
            pl.BlockSpec((TOK, TILE), lambda n: (0, n)),
            pl.BlockSpec((1, COLS, TILE), lambda n: (0, 0, n)),
        ],
        out_specs=pl.BlockSpec((COLS, TILE), lambda n: (0, n)),
        compiler_params=pltpu.CompilerParams(vmem_limit_bytes=32 * 2**20),
        cost_estimate=pl.CostEstimate(
            flops=2 * 10**9, bytes_accessed=13 * 10**6, transcendentals=0
        ),
    )(acts_t, other_side, err)


def right_kernel(place, left, gain_tail, mats_out, mats_value, own, other):
    chip, core = place[0], place[1]
    step = pl.program_id(0)
    lanes = pl.ds(pl.multiple_of(step * TILE, TILE), TILE)

    def put(side, span, value):
        for block in range(4):
            rows = pl.ds(pl.multiple_of(lax.rem(block - chip + 4, 4) * 8, 8), 8)
            part = value[block * 8 : (block + 1) * 8]

            @pl.when(core == side)
            def _():
                own[rows, span] = part

            @pl.when(core != side)
            def _():
                other[rows, span] = part

    for side, mats in enumerate((mats_out, mats_value)):
        rows = left[pl.ds(side * RANK, RANK), :]
        high, low = split2(rows)
        mats_high, mats_low = split2(mats[...])
        product = dot(high, mats_high) + (dot(low, mats_high) + dot(high, mats_low))
        put(side, lanes, product)

        @pl.when(step == 0)
        def _():
            gram = dot_split(rows, rows, ((1,), (1,)))
            wide = jnp.concatenate([gram, jnp.zeros((RANK, TAIL - RANK), F32)], axis=1)
            put(side, pl.ds(D, TAIL), wide + gain_tail[side])


def right_terms(place, left, gain_tail, mats_out, mats_value):
    whole = pl.BlockSpec((RANK, WIDE), lambda n: (0, 0))
    mats = pl.BlockSpec((COLS, TILE), lambda n: (0, n))
    return pl.pallas_call(
        right_kernel,
        name="right_terms",
        grid=(STEPS,),
        out_shape=(jax.ShapeDtypeStruct((RANK, WIDE), F32),) * 2,
        in_specs=[
            SMEM,
            pl.BlockSpec((2 * RANK, COLS), lambda n: (0, 0)),
            pl.BlockSpec((2, RANK, TAIL), lambda n: (0, 0, 0)),
            mats,
            mats,
        ],
        out_specs=(whole, whole),
        compiler_params=pltpu.CompilerParams(vmem_limit_bytes=32 * 2**20),
        cost_estimate=pl.CostEstimate(
            flops=1 * 10**9, bytes_accessed=9 * 10**6, transcendentals=0
        ),
    )(place, left, gain_tail, mats_out, mats_value)


def inverse_factor(gram):
    row_ids = lax.broadcasted_iota(jnp.int32, (RANK, 2 * RANK), 0)
    col_ids = lax.broadcasted_iota(jnp.int32, (RANK, 2 * RANK), 1)
    unit = jnp.where(row_ids + RANK == col_ids, 1.0, 0.0)
    work = jnp.concatenate([gram, jnp.zeros((RANK, RANK), F32)], axis=1) + unit
    for step in range(RANK - 1):
        pivot_row = work[step : step + 1, :]
        ratio = work[:, step : step + 1] / pivot_row[:, step : step + 1]
        work = work - jnp.where(row_ids > step, ratio * pivot_row, 0.0)
    diagonal = jnp.sum(jnp.where(row_ids == col_ids, work, 0.0), axis=1, keepdims=True)
    return work[:, RANK:] * lax.rsqrt(diagonal)


def finish_kernel(
    place, ours, theirs, left, mats_out, mats_value,
    err_out, err_value, right, ortho_out, tail_out,
    sums, ortho_parts, inverse,
):
    chip, core = place[0], place[1]
    step = pl.program_id(0)
    lanes = pl.ds(pl.multiple_of(step * TILE, TILE), TILE)

    @pl.when(step == 0)
    def _():
        for block in range(4):
            offset = lax.rem(chip + block, 4) * 8
            for side, source in ((core, ours), (1 - core, theirs)):
                rows = pl.ds(pl.multiple_of(side * RANK + offset, 8), 8)
                sums[rows, :] = source[pl.ds(block * 8, 8), :]
        tail_out[...] = sums[:, pl.ds(D, TAIL)]
        for side in range(2):
            span = pl.ds(side * RANK, RANK)
            gram = sums[span, pl.ds(D, TAIL)][:, :RANK] * (1.0 / WORKERS)
            factor = inverse_factor(gram)
            inverse[side] = factor
            ortho = dot_split(factor, left[span, :])
            ortho_out[span, :] = ortho * math.sqrt(HH)
            high, low = split2(ortho)
            parts = jnp.concatenate([high, low, high, jnp.zeros_like(high)], axis=0)
            ortho_parts[side] = parts.T

    for side, (mats, err) in enumerate(((mats_out, err_out), (mats_value, err_value))):
        span = pl.ds(side * RANK, RANK)
        rows = dot_split(inverse[side], sums[span, lanes]) * (1.0 / WORKERS)
        right[span, :] = rows
        high, low = split2(rows)
        parts = jnp.concatenate([high, high, low, jnp.zeros_like(high)], axis=0)
        err[0] = mats[...] - dot(ortho_parts[side], parts)


def finish(place, ours, theirs, left, mats_out, mats_value):
    whole = pl.BlockSpec((RANK, WIDE), lambda n: (0, 0))
    mats = pl.BlockSpec((COLS, TILE), lambda n: (0, n))
    err = pl.BlockSpec((1, COLS, TILE), lambda n: (0, 0, n))
    return pl.pallas_call(
        finish_kernel,
        name="finish",
        grid=(STEPS,),
        out_shape=(
            jax.ShapeDtypeStruct((1, COLS, D), F32),
            jax.ShapeDtypeStruct((1, COLS, D), F32),
            jax.ShapeDtypeStruct((2 * RANK, D), F32),
            jax.ShapeDtypeStruct((2 * RANK, COLS), F32),
            jax.ShapeDtypeStruct((2 * RANK, TAIL), F32),
        ),
        in_specs=[
            SMEM, whole, whole, pl.BlockSpec((2 * RANK, COLS), lambda n: (0, 0)), mats, mats,
        ],
        out_specs=(
            err,
            err,
            pl.BlockSpec((2 * RANK, TILE), lambda n: (0, n)),
            pl.BlockSpec((2 * RANK, COLS), lambda n: (0, 0)),
            pl.BlockSpec((2 * RANK, TAIL), lambda n: (0, 0)),
        ),
        scratch_shapes=[
            pltpu.VMEM((2 * RANK, WIDE), F32),
            pltpu.VMEM((2, COLS, 4 * RANK), BF16),
            pltpu.VMEM((2, RANK, RANK), F32),
        ],
        compiler_params=pltpu.CompilerParams(vmem_limit_bytes=32 * 2**20),
        cost_estimate=pl.CostEstimate(
            flops=1 * 10**9, bytes_accessed=17 * 10**6, transcendentals=0
        ),
    )(place, ours, theirs, left, mats_out, mats_value)


def to_core(value):
    return lax.ppermute(value, "tensor", [(i, i ^ 1) for i in range(8)])


def to_x(value, hops):
    return lax.ppermute(value, "tensor", [(i, (i // 2 + hops) % 4 * 2 + i % 2) for i in range(8)])


def to_z(value, hops):
    return lax.ppermute(value, "dp", [(i, i // 4 * 4 + (i + hops) % 4) for i in range(16)])


def to_y(value, hops):
    return lax.ppermute(value, "dp", [(i, (i // 4 + hops) % 4 * 4 + i % 4) for i in range(16)])


def ring_sum(value, send):
    opposite, after, before = send(value, 2), send(value, 1), send(value, 3)
    wide = value.astype(F32)
    return (wide + opposite.astype(F32)) + (after.astype(F32) + before.astype(F32))


def local(
    hidden_in, ln_gain, attn_probs, w_value, w_out, out_grad, err_out, err_value, factor_codes
):
    index = lax.axis_index("tensor")
    place = jnp.stack([index // 2, index % 2]).astype(jnp.int32)
    gain_row = ln_gain.reshape(1, D)
    normed, mixed_t, d_values_t, left_term = front(
        factor_codes, gain_row, hidden_in, attn_probs, w_value, w_out, out_grad, err_out, err_value
    )

    left = ring_sum(left_term, to_z)
    left = ring_sum(left.astype(BF16), to_y)

    own, other, gain_part = branch(place, d_values_t, w_value, normed, gain_row)
    mats_out = mats_of(mixed_t, out_grad, err_out, "mats_out")
    mats_value = mats_of(d_values_t, normed, err_value, "mats_value")

    chip_sum = (own.astype(F32) + to_core(other).astype(F32)).astype(BF16)
    far_after = to_x(chip_sum[2, :64], 1)
    far_before = to_x(chip_sum[2, 64:], 3)
    next_part = chip_sum[1].astype(F32).at[:64].add(far_after.astype(F32)).astype(BF16)
    last_part = chip_sum[3].astype(F32).at[64:].add(far_before.astype(F32)).astype(BF16)
    total = chip_sum[0].astype(F32) + (
        to_x(next_part, 1).astype(F32) + to_x(last_part, 3).astype(F32)
    )
    hidden = lax.dynamic_slice_in_dim(hidden_in, index * 128, 128, 0).astype(F32)
    centred = hidden - jnp.mean(hidden, axis=-1, keepdims=True)
    inv_std = lax.rsqrt(jnp.mean(centred * centred, axis=-1, keepdims=True) + 1e-05)
    standard = centred * inv_std
    scaled = total * ln_gain
    first_mean = jnp.mean(scaled, axis=-1, keepdims=True)
    second_mean = jnp.mean(scaled * standard, axis=-1, keepdims=True)
    in_grad = (inv_std * (scaled - first_mean - standard * second_mean)).astype(BF16)

    gain_tail = jnp.pad(gain_part.reshape(2, RANK, 40), ((0, 0), (0, 0), (RANK, TAIL - RANK - 40)))
    ours, theirs = right_terms(place, left, gain_tail, mats_out, mats_value)
    chunks = ours + to_core(theirs)
    opposite, after, before = (to_x(chunks[8 * k : 8 * k + 8], k) for k in (2, 1, 3))
    chunk = (chunks[:8] + opposite) + (after + before)
    chunk = ring_sum(chunk, to_z)
    chunk = ring_sum(chunk, to_y)
    opposite, after, before = to_x(chunk, 2), to_x(chunk, 3), to_x(chunk, 1)
    ours = jnp.concatenate([chunk, after, opposite, before], axis=0)
    theirs = to_core(ours)
    new_out, new_value, right, ortho, tail = finish(place, ours, theirs, left, mats_out, mats_value)
    gain_grad = tail[:, RANK : RANK + 40].reshape(D)
    share = lax.dynamic_slice_in_dim(right, index * (D // 8), D // 8, 1)
    return (
        in_grad,
        gain_grad,
        new_out,
        new_value,
        ortho[:RANK].T,
        ortho[RANK:].T,
        share[:RANK].T,
        share[RANK:].T,
    )


def solution(mesh):
    in_specs = (
        P("dp", None),
        P(),
        P("dp", "tensor", None, None),
        P(None, "tensor"),
        P("tensor", None),
        P("dp", None),
        P("dp", "tensor", None),
        P("dp", "tensor", None),
        P(),
    )
    out_specs = (
        P(("dp", "tensor"), None),
        P(),
        P("dp", "tensor", None),
        P("dp", "tensor", None),
        P("tensor", None),
        P("tensor", None),
        P("tensor", None),
        P("tensor", None),
    )
    return jax.shard_map(local, mesh=mesh, in_specs=in_specs, out_specs=out_specs, check_vma=False)
```

```python
import math

import jax
import jax.numpy as jnp
from jax import lax
from jax.experimental import pallas as pl
from jax.experimental.pallas import tpu as pltpu
from jax.sharding import PartitionSpec as P

D = 2560
RANK = 32
HEADS = 24
HEAD_DIM = 128
LEN = 512
CROPS = 2
HEADS_DEV = 3
TOK = CROPS * LEN
COLS = HEADS_DEV * HEAD_DIM
HH = HEADS * HEAD_DIM
SENT = D + 128
WIDE = D + 384
TILE = 512
STEPS = D // TILE
LN_ROWS = 512
MERGE = 2
WORKERS = 16
F32 = jnp.float32
BF16 = jnp.bfloat16
ANY = pl.BlockSpec(memory_space=pl.ANY)
SMEM = pl.BlockSpec(memory_space=pltpu.SMEM)


def place():
    index = lax.axis_index("tensor")
    return lax.div(index, 2), lax.rem(index, 2)


def dot(a, b, dims=((1,), (0,))):
    return lax.dot_general(a, b, (dims, ((), ())), preferred_element_type=F32)


def split2(a):
    high = a.astype(BF16)
    return high, (a - high.astype(F32)).astype(BF16)


def dot_split(a, b, dims=((1,), (0,))):
    a_high, a_low = split2(a)
    b_high, b_low = split2(b)
    return dot(a_high, b_high, dims) + (dot(a_low, b_high, dims) + dot(a_high, b_low, dims))


def lane_parts(value, group):
    high = value.astype(BF16).astype(F32)
    rest = value - high
    middle = rest.astype(BF16).astype(F32)
    low = rest - middle
    zero = jnp.zeros_like(value)
    return jnp.where(
        group == 0, high, jnp.where(group == 1, middle, jnp.where(group == 2, low, zero))
    ).astype(BF16)


def start_rows(code, first, rows):
    row_ids = lax.broadcasted_iota(jnp.int32, (rows, 128), 0) + first
    lane = lax.broadcasted_iota(jnp.int32, (rows, 128), 1)
    hashed = row_ids * 40503 + jnp.bitwise_and(lane, RANK - 1) * 1531 + code * 7919
    hashed = jnp.bitwise_xor(hashed, jnp.right_shift(hashed, 15)) * 668265261
    hashed = jnp.bitwise_xor(hashed, jnp.right_shift(hashed, 15)) * 374761393
    hashed = jnp.bitwise_xor(hashed, jnp.right_shift(hashed, 13))
    level = jnp.bitwise_and(hashed, 8388607).astype(F32)
    start = ((level + 0.5) / 8388608.0 - 0.5) * math.sqrt(12.0)
    return lane_parts(start, jnp.right_shift(lane, 5))


def norm_rows(hidden, gain, first, count):
    blocks = [pl.ds(pl.multiple_of(first + 32 * block, 32), 32) for block in range(count)]
    spans = [pl.ds(part * 128, 128) for part in range(D // 128)]
    means, scales = [], []
    for rows in blocks:
        total = hidden[rows, spans[0]].astype(F32)
        for span in spans[1:]:
            total = total + hidden[rows, span].astype(F32)
        means.append(jnp.sum(total, axis=1, keepdims=True) * (1.0 / D))
    for rows, mean in zip(blocks, means):
        total = jnp.zeros((32, 128), F32)
        for span in spans:
            centred = hidden[rows, span].astype(F32) - mean
            total = total + centred * centred
        scales.append(lax.rsqrt(jnp.sum(total, axis=1, keepdims=True) * (1.0 / D) + 1e-05))
    for rows, mean, scale in zip(blocks, means, scales):
        for span in spans:
            centred = hidden[rows, span].astype(F32) - mean
            hidden[rows, span] = (centred * scale * gain[:, span]).astype(BF16)


def front_kernel(
    codes, gain, hidden, probs, w_value, w_out, out_grad, err_out, err_value,
    mats_out, mats_value, left_out, own_half, other_half, gain_out, hidden_rows,
    hidden_v, probs_v, w_value_v, w_value_t, w_out_v, grad_v, err_out_v, err_value_v,
    starts, values_t, d_mixed_t, mixed_t, d_values_t, mats_out_v, mats_value_v, left_sum, gain_v,
    codes_v, gain_flat, gain_row, sems, out_sems, small_sems,
):
    half = TOK // 2
    halves = [pl.ds(part * half, half) for part in range(2)]
    pairs = (
        (hidden.at[halves[0]], hidden_v.at[halves[0]]),
        (w_out, w_out_v),
        (out_grad.at[halves[0]], grad_v.at[halves[0]]),
        (hidden.at[halves[1]], hidden_v.at[halves[1]]),
        (out_grad.at[halves[1]], grad_v.at[halves[1]]),
        (w_value, w_value_v),
        (probs, probs_v),
        (err_out.at[0], err_out_v),
        (err_value.at[0], err_value_v),
    )
    copies = [
        pltpu.make_async_copy(source, target, sems.at[index])
        for index, (source, target) in enumerate(pairs)
    ]
    small = (
        pltpu.make_async_copy(codes, codes_v, small_sems.at[0]),
        pltpu.make_async_copy(gain, gain_flat, small_sems.at[1]),
    )
    for copy in small:
        copy.start()
    for copy in copies[:4]:
        copy.start()
    index = lax.axis_index("tensor")
    rows_copy = pltpu.make_async_copy(
        hidden.at[pl.ds(pl.multiple_of(index * 128, 128), 128)], hidden_rows, out_sems.at[2 * STEPS]
    )

    def d_mixed_of(rows):
        d_mixed_t[:, rows] = dot(w_out_v[...], grad_v[rows, :], ((1,), (1,))).astype(BF16)

    for copy in small:
        copy.wait()
    @pl.loop(0, D // 128)
    def _(step):
        rows = pl.ds(pl.multiple_of(step * 128, 128), 128)
        for side in range(2):
            starts[side, rows, :] = start_rows(codes_v[side], step * 128, 128)

    for part in range(D // 128):
        span = pl.ds(part * 128, 128)
        gain_row[:, span] = gain_flat[span].reshape(1, 128)
    copies[0].wait()

    @pl.loop(0, half // LN_ROWS)
    def _(step):
        norm_rows(hidden_v, gain_row, step * LN_ROWS, LN_ROWS // 32)

    for copy in copies[4:6]:
        copy.start()
    for copy in copies[1:4]:
        copy.wait()
    for copy in copies[6:]:
        copy.start()
    rows_copy.start()

    @pl.loop(0, MERGE)
    def _(step):
        size = half // MERGE
        norm_rows(hidden_v, gain_row, half + step * size, size // 32)
        d_mixed_of(pl.ds(pl.multiple_of(step * size, size), size))

    for copy in copies[4:6]:
        copy.wait()

    @pl.loop(0, 2)
    def _(step):
        size = half // 2
        d_mixed_of(pl.ds(pl.multiple_of(half + step * size, size), size))
        for block in range(5):
            span = pl.ds(pl.multiple_of(step * 1280 + block * 256, 256), 256)
            w_value_t[:, span] = w_value_v[span, :].T

    for rows in halves:
        values_t[:, rows] = dot(w_value_t[...], hidden_v[rows, :], ((1,), (1,))).astype(BF16)

    copies[6].wait()
    for crop in range(CROPS):
        rows = pl.ds(crop * LEN, LEN)
        for head in range(HEADS_DEV):
            cols = pl.ds(head * HEAD_DIM, HEAD_DIM)
            weights = probs_v[crop, head]
            mixed_t[cols, rows] = dot(values_t[cols, rows], weights, ((1,), (1,))).astype(BF16)
            d_values_t[cols, rows] = dot(d_mixed_t[cols, rows], weights).astype(BF16)

    chip, core = place()
    for block in range(8):
        slot = pl.ds(pl.multiple_of(lax.rem(block // 2 - chip + 4, 4) * 128, 128), 128)
        part = d_values_t[:, pl.ds(block * 128, 128)]

        @pl.when(core == block % 2)
        def _():
            own_half[:, slot] = part

        @pl.when(core != block % 2)
        def _():
            other_half[:, slot] = part

    sides = (
        (copies[7], mixed_t, grad_v, err_out_v, mats_out_v, mats_out),
        (copies[8], d_values_t, hidden_v, err_value_v, mats_value_v, mats_value),
    )

    def write(index, step):
        span = pl.ds(step * TILE, TILE)
        mats_v, mats = sides[index][4:]
        return pltpu.make_async_copy(
            mats_v.at[:, span], mats.at[:, span], out_sems.at[index * STEPS + step]
        )

    for index, (copy, acts_t, other_side, err_v, mats_v, mats) in enumerate(sides):
        copy.wait()
        left_sum[...] = jnp.zeros((COLS, 128), F32)

        for step in range(STEPS):
            span = pl.ds(step * TILE, TILE)
            grad = dot(acts_t[...], other_side[:, span])
            rounded = (grad + err_v[:, span]).astype(BF16)
            mats_v[:, span] = rounded
            write(index, step).start()
            left_sum[...] += dot(rounded, starts[index, span, :])
            if index == 1:
                turned = w_value_t[:, span].astype(F32)
                gain_v[:, span] = jnp.sum(grad * turned, axis=0, keepdims=True) / gain_row[:, span]

        turned = left_sum[...].T
        left_out[pl.ds(index * RANK, RANK), :] = (
            turned[0:32] + (turned[32:64] + turned[64:96])
        ).astype(BF16)
    gain_out[...] = jnp.zeros((2 * RANK, 128), F32)
    for part in range(D // 128):
        gain_out[pl.ds(part // 3 * 8 + part % 3, 1), :] = gain_v[:, pl.ds(part * 128, 128)]

    for step in range(STEPS):
        for index in range(2):
            write(index, step).wait()
    rows_copy.wait()


def front(codes, gain, hidden, probs, w_value, w_out, out_grad, err_out, err_value):
    vmem = pl.BlockSpec(memory_space=pltpu.VMEM)
    return pl.pallas_call(
        front_kernel,
        name="front",
        out_shape=(
            jax.ShapeDtypeStruct((COLS, D), BF16),
            jax.ShapeDtypeStruct((COLS, D), BF16),
            jax.ShapeDtypeStruct((2 * RANK, COLS), BF16),
            jax.ShapeDtypeStruct((COLS, TOK // 2), BF16),
            jax.ShapeDtypeStruct((COLS, TOK // 2), BF16),
            jax.ShapeDtypeStruct((2 * RANK, 128), F32),
            jax.ShapeDtypeStruct((128, D), BF16),
        ),
        in_specs=[ANY] * 9,
        out_specs=(ANY, ANY, vmem, vmem, vmem, vmem, ANY),
        scratch_shapes=[
            pltpu.VMEM((TOK, D), BF16),
            pltpu.VMEM((CROPS, HEADS_DEV, LEN, LEN), BF16),
            pltpu.VMEM((D, COLS), BF16),
            pltpu.VMEM((COLS, D), BF16),
            pltpu.VMEM((COLS, D), BF16),
            pltpu.VMEM((TOK, D), BF16),
            pltpu.VMEM((COLS, D), F32),
            pltpu.VMEM((COLS, D), F32),
            pltpu.VMEM((2, D, 128), BF16),
            pltpu.VMEM((COLS, TOK), BF16),
            pltpu.VMEM((COLS, TOK), BF16),
            pltpu.VMEM((COLS, TOK), BF16),
            pltpu.VMEM((COLS, TOK), BF16),
            pltpu.VMEM((COLS, D), BF16),
            pltpu.VMEM((COLS, D), BF16),
            pltpu.VMEM((COLS, 128), F32),
            pltpu.VMEM((1, D), F32),
            pltpu.SMEM((2,), jnp.int32),
            pltpu.VMEM((D,), F32),
            pltpu.VMEM((1, D), F32),
            pltpu.SemaphoreType.DMA((9,)),
            pltpu.SemaphoreType.DMA((2 * STEPS + 1,)),
            pltpu.SemaphoreType.DMA((2,)),
        ],
        compiler_params=pltpu.CompilerParams(vmem_limit_bytes=48 * 2**20),
        cost_estimate=pl.CostEstimate(
            flops=11 * 10**9, bytes_accessed=32 * 10**6, transcendentals=0
        ),
    )(
        pltpu.with_memory_space_constraint(codes, pltpu.HBM),
        pltpu.with_memory_space_constraint(gain, pltpu.HBM),
        hidden, probs, w_value, w_out, out_grad, err_out, err_value,
    )


def branch_kernel(
    own_half, other_half, w_own, w_other, here, after, before, far_after, far_before, d_values
):
    @pl.when(pl.program_id(0) == 0)
    def _():
        for block in range(2):
            rows = pl.ds(block * 256, 256)
            d_values[rows, pl.ds(0, COLS)] = own_half[:, rows].T
            d_values[rows, pl.ds(COLS, COLS)] = other_half[:, rows].T

    weights = jnp.concatenate([w_own[...], w_other[...]], axis=1)
    product = dot(d_values[...], weights, ((1,), (1,))).astype(BF16)
    here[...] = product[0:128]
    after[...] = product[128:256]
    far_after[...] = product[256:320]
    far_before[...] = product[320:384]
    before[...] = product[384:512]


def branch(own_half, other_half, w_own, w_other):
    half = pl.BlockSpec((COLS, TOK // 2), lambda n: (0, 0))
    weights = pl.BlockSpec((1280, COLS), lambda n: (n, 0))
    rows = (128, 128, 128, 64, 64)
    return pl.pallas_call(
        branch_kernel,
        name="branch",
        grid=(2,),
        out_shape=[jax.ShapeDtypeStruct((count, D), BF16) for count in rows],
        in_specs=[half, half, weights, weights],
        out_specs=[pl.BlockSpec((count, 1280), lambda n: (0, n)) for count in rows],
        scratch_shapes=[pltpu.VMEM((TOK // 2, 2 * COLS), BF16)],
        compiler_params=pltpu.CompilerParams(vmem_limit_bytes=20 * 2**20),
        cost_estimate=pl.CostEstimate(
            flops=2 * 10**9, bytes_accessed=7 * 10**6, transcendentals=0
        ),
    )(
        own_half,
        other_half,
        pltpu.with_memory_space_constraint(w_own, pltpu.HBM),
        pltpu.with_memory_space_constraint(w_other, pltpu.HBM),
    )


def relay_kernel(after, before, far_after, far_before, next_after, next_before):
    top, low = pl.ds(0, 64), pl.ds(64, 64)
    next_after[top, :] = (after[top, :].astype(F32) + far_after[...].astype(F32)).astype(BF16)
    next_after[low, :] = after[low, :]
    next_before[top, :] = before[top, :]
    next_before[low, :] = (before[low, :].astype(F32) + far_before[...].astype(F32)).astype(BF16)


def relay(after, before, far_after, far_before):
    whole = pl.BlockSpec((128, 2560), lambda n: (0, n))
    part = pl.BlockSpec((64, 2560), lambda n: (0, n))
    return pl.pallas_call(
        relay_kernel,
        name="relay",
        grid=(1,),
        out_shape=(jax.ShapeDtypeStruct((128, D), BF16),) * 2,
        in_specs=[whole, whole, part, part],
        out_specs=(whole, whole),
        compiler_params=pltpu.CompilerParams(vmem_limit_bytes=8 * 2**20),
        cost_estimate=pl.CostEstimate(
            flops=10**6, bytes_accessed=4 * 10**6, transcendentals=0
        ),
    )(after, before, far_after, far_before)


def norm_back_kernel(hidden, gain, here, after, before, in_grad, total, standard):
    spans = [pl.ds(part * 128, 128) for part in range(D // 128)]
    for block in range(4):
        rows = pl.ds(block * 32, 32)
        mean = jnp.zeros((32, 128), F32)
        for span in spans:
            mean = mean + hidden[rows, span].astype(F32)
        mean = jnp.sum(mean, axis=1, keepdims=True) * (1.0 / D)
        square = jnp.zeros((32, 128), F32)
        for span in spans:
            centred = hidden[rows, span].astype(F32) - mean
            square = square + centred * centred
        inv_std = lax.rsqrt(jnp.sum(square, axis=1, keepdims=True) * (1.0 / D) + 1e-05)
        first = jnp.zeros((32, 128), F32)
        second = jnp.zeros((32, 128), F32)
        for span in spans:
            summed = here[rows, span].astype(F32) + (
                after[rows, span].astype(F32) + before[rows, span].astype(F32)
            )
            scaled = summed * gain[:, span]
            unit = (hidden[rows, span].astype(F32) - mean) * inv_std
            total[rows, span] = scaled
            standard[rows, span] = unit
            first = first + scaled
            second = second + scaled * unit
        first = jnp.sum(first, axis=1, keepdims=True) * (1.0 / D)
        second = jnp.sum(second, axis=1, keepdims=True) * (1.0 / D)
        for span in spans:
            in_grad[rows, span] = (
                inv_std * (total[rows, span] - first - standard[rows, span] * second)
            ).astype(BF16)


def norm_back(hidden, gain, here, after, before):
    rows = pl.BlockSpec((128, D), lambda n: (n, 0))
    return pl.pallas_call(
        norm_back_kernel,
        name="norm_back",
        grid=(1,),
        in_specs=[rows, pl.BlockSpec((1, D), lambda n: (0, 0)), rows, rows, rows],
        out_specs=rows,
        scratch_shapes=[pltpu.VMEM((128, D), F32), pltpu.VMEM((128, D), F32)],
        out_shape=jax.ShapeDtypeStruct((128, D), BF16),
        compiler_params=pltpu.CompilerParams(vmem_limit_bytes=16 * 2**20),
        cost_estimate=pl.CostEstimate(
            flops=5 * 10**6, bytes_accessed=10**6, transcendentals=0
        ),
    )(hidden, gain, here, after, before)


def right_kernel(left, gain_rows, mats_out, mats_value, own, other, staged):
    chip, core = place()
    step = pl.program_id(0)
    lanes = pl.ds(pl.multiple_of(step * 2560, 2560), 2560)

    def put(side, span, value):
        for block in range(4):
            rows = pl.ds(pl.multiple_of(lax.rem(block - chip + 4, 4) * 8, 8), 8)
            part = value[block * 8 : (block + 1) * 8]

            @pl.when(core == side)
            def _():
                own[rows, span] = part

            @pl.when(core != side)
            def _():
                staged[rows, span] = part

    for side, mats in enumerate((mats_out, mats_value)):
        span = pl.ds(side * RANK, RANK)
        rows = left[span, :]
        parts = jnp.concatenate(split2(rows), axis=0)
        product = dot(parts, mats[...])
        put(side, lanes, product[:RANK] + product[RANK:])

        @pl.when(step == 0)
        def _():
            gram = dot_split(rows, rows, ((1,), (1,)))
            packed = jnp.concatenate([gram[8 * k : 8 * k + 8] for k in range(4)], axis=1)
            put(side, pl.ds(D, 128), gain_rows[span, :])
            high, low = split2(packed)
            for place_at, part in ((SENT, high), (SENT + 128, low)):
                put(side, pl.ds(place_at, 128), jnp.concatenate([part.astype(F32)] * 4, axis=0))

    @pl.when(step == 0)
    def _():
        other[...] = staged[...].astype(BF16)


def right_terms(left, gain_rows, mats_out, mats_value):
    whole = pl.BlockSpec((RANK, WIDE), lambda n: (0, 0))
    mats = pl.BlockSpec((COLS, 2560), lambda n: (0, n))
    return pl.pallas_call(
        right_kernel,
        name="right_terms",
        grid=(1,),
        out_shape=(
            jax.ShapeDtypeStruct((RANK, WIDE), F32),
            jax.ShapeDtypeStruct((RANK, WIDE), BF16),
        ),
        in_specs=[
            pl.BlockSpec((2 * RANK, COLS), lambda n: (0, 0)),
            pl.BlockSpec((2 * RANK, 128), lambda n: (0, 0)),
            mats,
            mats,
        ],
        out_specs=(whole, whole),
        scratch_shapes=[pltpu.VMEM((RANK, WIDE), F32)],
        compiler_params=pltpu.CompilerParams(vmem_limit_bytes=16 * 2**20),
        cost_estimate=pl.CostEstimate(
            flops=5 * 10**8, bytes_accessed=5 * 10**6, transcendentals=0
        ),
    )(left, gain_rows, mats_out, mats_value)


def factor_kernel(packed, inverse):
    whole = packed[:, pl.ds(0, 128)] + packed[:, pl.ds(128, 128)]
    gram = jnp.concatenate([whole[:, k * RANK : (k + 1) * RANK] for k in range(4)], axis=0)
    row_ids = lax.broadcasted_iota(jnp.int32, (RANK, 128), 0)
    col_ids = lax.broadcasted_iota(jnp.int32, (RANK, 128), 1)
    unit = jnp.where(row_ids + RANK == col_ids, 1.0, 0.0)
    work = unit + jnp.concatenate([gram, jnp.zeros((RANK, 128 - RANK), F32)], axis=1)
    for step in range(0, RANK, 2):
        first, second = work[step : step + 1, :], work[step + 1 : step + 2, :]
        column = jnp.broadcast_to(work[:, step : step + 1], (RANK, 128))
        other = jnp.broadcast_to(work[:, step + 1 : step + 2], (RANK, 128))
        scale = 1.0 / column[step : step + 1, :]
        ratio = other[step : step + 1, :] * scale
        other = other - column * ratio
        second = second - first * ratio
        after = row_ids > step + 1
        work = jnp.where(row_ids == step + 1, second, work) - jnp.where(
            after,
            column * (first * scale) + other * (second / other[step + 1 : step + 2, :]),
            0.0,
        )
    diagonal = jnp.sum(jnp.where(row_ids == col_ids, work, 0.0), axis=1, keepdims=True)
    scaled = work * lax.rsqrt(diagonal)
    high, low = split2(pltpu.roll(scaled, 128 - RANK, 1))
    inverse[:, pl.ds(0, 128)] = high
    inverse[:, pl.ds(128, 128)] = low


def factor(packed):
    return pl.pallas_call(
        factor_kernel,
        name="factor",
        out_shape=jax.ShapeDtypeStruct((RANK, 256), BF16),
        cost_estimate=pl.CostEstimate(
            flops=5 * 10**6, bytes_accessed=3 * 10**6, transcendentals=0
        ),
    )(packed)


def finish_kernel(
    ours, theirs, left, mats_out, mats_value,
    err_out, err_value, share_out, share_value, ortho_out, ortho_value, gain_out,
    sums, ortho_parts, right,
):
    chip, core = place()
    step = pl.program_id(0)
    lanes = pl.ds(pl.multiple_of(step * 1280, 1280), 1280)

    @pl.when(step == 0)
    def _():
        for side, source in ((core, ours), (1 - core, theirs)):
            wide = source[...].astype(F32)
            for block in range(4):
                offset = lax.rem(chip + block, 4) * 8
                rows = pl.ds(pl.multiple_of(side * RANK + offset, 8), 8)
                sums[rows, pl.ds(0, SENT)] = wide[block * 8 : block * 8 + 8, :SENT]
            rows = pl.ds(pl.multiple_of(side * RANK, RANK), RANK)
            sums[rows, pl.ds(SENT, 128)] = wide[:, SENT : SENT + 128] + wide[:, SENT + 128 :]
        for part in range(D // 128):
            gain_out[:, pl.ds(part * 128, 128)] = sums[
                pl.ds(part // 3 * 8 + part % 3, 1), pl.ds(D, 128)
            ]
        for side, scaled in enumerate((ortho_out, ortho_value)):
            span = pl.ds(side * RANK, RANK)
            inverse = sums[span, pl.ds(SENT, 128)][:, :RANK]
            ortho = dot_split(inverse, left[span, :])
            scaled[...] = ortho * math.sqrt(HH)
            high, low = split2(ortho)
            parts = jnp.concatenate([high, low, high, jnp.zeros_like(high)], axis=0)
            ortho_parts[side] = parts.T

    for side, (mats, err) in enumerate(((mats_out, err_out), (mats_value, err_value))):
        span = pl.ds(side * RANK, RANK)
        inverse = sums[span, pl.ds(SENT, 128)][:, :RANK]
        rows = dot_split(inverse, sums[span, lanes]) * (1.0 / WORKERS)
        right[span, lanes] = rows
        high, low = split2(rows)
        parts = jnp.concatenate([high, high, low, jnp.zeros_like(high)], axis=0)
        err[0] = mats[...].astype(F32) - dot(ortho_parts[side], parts)

    @pl.when(step == 1)
    def _():
        index = chip * 2 + core
        window = right[:, pl.ds(pl.multiple_of(index * 5 // 2 * 128, 128), 512)]
        window = jnp.where(lax.rem(index, 2) == 1, pltpu.roll(window, 512 - 64, 1), window)
        share_out[...] = window[:RANK, : D // 8]
        share_value[...] = window[RANK:, : D // 8]


def finish(ours, theirs, left, mats_out, mats_value):
    whole = pl.BlockSpec((RANK, WIDE), lambda n: (0, 0))
    mats = pl.BlockSpec((COLS, 1280), lambda n: (0, n))
    err = pl.BlockSpec((1, COLS, 1280), lambda n: (0, 0, n))
    share = pl.BlockSpec((RANK, D // 8), lambda n: (0, 0))
    ortho = pl.BlockSpec((RANK, COLS), lambda n: (0, 0))
    return pl.pallas_call(
        finish_kernel,
        name="finish",
        grid=(2,),
        out_shape=(
            jax.ShapeDtypeStruct((1, COLS, D), F32),
            jax.ShapeDtypeStruct((1, COLS, D), F32),
            jax.ShapeDtypeStruct((RANK, D // 8), F32),
            jax.ShapeDtypeStruct((RANK, D // 8), F32),
            jax.ShapeDtypeStruct((RANK, COLS), F32),
            jax.ShapeDtypeStruct((RANK, COLS), F32),
            jax.ShapeDtypeStruct((1, D), F32),
        ),
        in_specs=[
            whole, whole, pl.BlockSpec((2 * RANK, COLS), lambda n: (0, 0)), mats, mats,
        ],
        out_specs=(
            err, err, share, share, ortho, ortho, pl.BlockSpec((1, D), lambda n: (0, 0)),
        ),
        scratch_shapes=[
            pltpu.VMEM((2 * RANK, WIDE), F32),
            pltpu.VMEM((2, COLS, 4 * RANK), BF16),
            pltpu.VMEM((2 * RANK, WIDE), F32),
        ],
        compiler_params=pltpu.CompilerParams(vmem_limit_bytes=20 * 2**20),
        cost_estimate=pl.CostEstimate(
            flops=1 * 10**9, bytes_accessed=13 * 10**6, transcendentals=0
        ),
    )(ours, theirs, left, mats_out, mats_value)


def to_core(value):
    return lax.ppermute(value, "tensor", [(i, i ^ 1) for i in range(8)])


def to_x(value, hops):
    return lax.ppermute(value, "tensor", [(i, (i // 2 + hops) % 4 * 2 + i % 2) for i in range(8)])


def to_z(value, hops):
    return lax.ppermute(value, "dp", [(i, i // 4 * 4 + (i + hops) % 4) for i in range(16)])


def to_y(value, hops):
    return lax.ppermute(value, "dp", [(i, (i // 4 + hops) % 4 * 4 + i % 4) for i in range(16)])


def rounded(value):
    return lax.reduce_precision(value, 8, 7).astype(BF16)


def ring_sum(value, send):
    opposite, after, before = send(value, 2), send(value, 1), send(value, 3)
    wide = value.astype(F32)
    return (wide + opposite.astype(F32)) + (after.astype(F32) + before.astype(F32))


def local(
    hidden_in, ln_gain, attn_probs, w_value, w_out, out_grad, err_out, err_value, factor_codes
):
    gain_row = ln_gain.reshape(1, D)
    w_other = to_core(w_value)
    mats_out, mats_value, left_term, own_half, other_half, gain_rows, hidden_rows = front(
        factor_codes, ln_gain, hidden_in, attn_probs, w_value, w_out, out_grad,
        err_out, err_value,
    )
    received_half = to_core(other_half)

    left = ring_sum(left_term, to_z)
    here, after, before, far_after, far_before = branch(own_half, received_half, w_value, w_other)
    left_term, far_after, far_before = lax.optimization_barrier(
        (rounded(left), far_after, far_before)
    )
    far_after, far_before = to_x(far_after, 1), to_x(far_before, 3)
    passes = 1 + lax.axis_index("dp") // WORKERS

    def sum_left(step, carry):
        left = ring_sum(carry[0], to_y)
        return rounded(left), left

    _, left = lax.fori_loop(
        0, passes, sum_left, (left_term, jnp.zeros((2 * RANK, COLS), F32))
    )
    left, far_after, far_before = lax.optimization_barrier((left, far_after, far_before))

    ours, theirs = right_terms(left, gain_rows, mats_out, mats_value)
    chunks = ours + to_core(theirs).astype(F32)
    next_after, next_before = relay(after, before, far_after, far_before)
    grams = chunks[:, SENT : SENT + 128] + chunks[:, SENT + 128 :]
    high = lax.reduce_precision(grams, 8, 7)
    chunks = jnp.concatenate([chunks[:, :SENT], high, grams - high], axis=1)
    opposite, after, before = (
        to_x(rounded(chunks[8 * k : 8 * k + 8]), k).astype(F32) for k in (2, 1, 3)
    )
    chunk = (chunks[:8] + opposite) + (after + before)
    packed = chunk[:, SENT:]
    chunk, next_after, next_before = lax.optimization_barrier(
        (rounded(chunk[:, :SENT]), next_after, next_before)
    )
    near_after, near_before = to_x(next_after, 1), to_x(next_before, 3)

    def over_workers(step, carry):
        chunk, _ = carry
        inverse = factor(packed)
        chunk = ring_sum(chunk, to_z)
        chunk, inverse = lax.optimization_barrier((chunk, inverse))
        return rounded(ring_sum(rounded(chunk), to_y)), inverse

    chunk, inverse = lax.fori_loop(
        0, passes, over_workers, (chunk, jnp.zeros((RANK, 256), BF16))
    )
    chunk, near_after, near_before = lax.optimization_barrier((chunk, near_after, near_before))
    in_grad = norm_back(hidden_rows, gain_row, here, near_after, near_before)
    opposite, after, before = to_x(chunk, 2), to_x(chunk, 3), to_x(chunk, 1)
    rows = jnp.concatenate([chunk, after, opposite, before], axis=0)
    ours = jnp.concatenate([rows, inverse], axis=1)
    theirs, in_grad = lax.optimization_barrier((to_core(ours), in_grad))
    new_out, new_value, share_out, share_value, ortho_out, ortho_value, gain_grad = finish(
        ours, theirs, left, mats_out, mats_value
    )
    return (
        in_grad,
        gain_grad.reshape(D),
        new_out,
        new_value,
        ortho_out.T,
        ortho_value.T,
        share_out.T,
        share_value.T,
    )


def solution(mesh):
    in_specs = (
        P("dp", None),
        P(),
        P("dp", "tensor", None, None),
        P(None, "tensor"),
        P("tensor", None),
        P("dp", None),
        P("dp", "tensor", None),
        P("dp", "tensor", None),
        P(),
    )
    out_specs = (
        P(("dp", "tensor"), None),
        P(),
        P("dp", "tensor", None),
        P("dp", "tensor", None),
        P("tensor", None),
        P("tensor", None),
        P("tensor", None),
        P("tensor", None),
    )
    return jax.shard_map(local, mesh=mesh, in_specs=in_specs, out_specs=out_specs, check_vma=False)
```

```python
import math

import jax
import jax.numpy as jnp
from jax import lax
from jax.experimental import pallas as pl
from jax.experimental.pallas import tpu as pltpu
from jax.sharding import PartitionSpec as P

D = 2560
RANK = 32
HEADS = 24
HEAD_DIM = 128
LEN = 512
CROPS = 2
HEADS_DEV = 3
TOK = CROPS * LEN
COLS = HEADS_DEV * HEAD_DIM
HH = HEADS * HEAD_DIM
SENT = D + 128
WIDE = D + 384
TILE = 512
STEPS = D // TILE
LN_ROWS = 512
MERGE = 2
WORKERS = 16
F32 = jnp.float32
BF16 = jnp.bfloat16
ANY = pl.BlockSpec(memory_space=pl.ANY)
SMEM = pl.BlockSpec(memory_space=pltpu.SMEM)


def place():
    index = lax.axis_index("tensor")
    return lax.div(index, 2), lax.rem(index, 2)


def dot(a, b, dims=((1,), (0,))):
    return lax.dot_general(a, b, (dims, ((), ())), preferred_element_type=F32)


def split2(a):
    high = a.astype(BF16)
    return high, (a - high.astype(F32)).astype(BF16)


def dot_split(a, b, dims=((1,), (0,))):
    a_high, a_low = split2(a)
    b_high, b_low = split2(b)
    return dot(a_high, b_high, dims) + (dot(a_low, b_high, dims) + dot(a_high, b_low, dims))


def lane_parts(value, group):
    high = value.astype(BF16).astype(F32)
    rest = value - high
    middle = rest.astype(BF16).astype(F32)
    low = rest - middle
    zero = jnp.zeros_like(value)
    return jnp.where(
        group == 0, high, jnp.where(group == 1, middle, jnp.where(group == 2, low, zero))
    ).astype(BF16)


def start_rows(code, first, rows):
    row_ids = lax.broadcasted_iota(jnp.int32, (rows, 128), 0) + first
    lane = lax.broadcasted_iota(jnp.int32, (rows, 128), 1)
    hashed = row_ids * 40503 + jnp.bitwise_and(lane, RANK - 1) * 1531 + code * 7919
    hashed = jnp.bitwise_xor(hashed, jnp.right_shift(hashed, 15)) * 668265261
    hashed = jnp.bitwise_xor(hashed, jnp.right_shift(hashed, 15)) * 374761393
    hashed = jnp.bitwise_xor(hashed, jnp.right_shift(hashed, 13))
    level = jnp.bitwise_and(hashed, 8388607).astype(F32)
    start = ((level + 0.5) / 8388608.0 - 0.5) * math.sqrt(12.0)
    return lane_parts(start, jnp.right_shift(lane, 5))


def norm_rows(hidden, gain, first, count):
    blocks = [pl.ds(pl.multiple_of(first + 32 * block, 32), 32) for block in range(count)]
    spans = [pl.ds(part * 128, 128) for part in range(D // 128)]
    means, scales = [], []
    for rows in blocks:
        total = hidden[rows, spans[0]].astype(F32)
        for span in spans[1:]:
            total = total + hidden[rows, span].astype(F32)
        means.append(jnp.sum(total, axis=1, keepdims=True) * (1.0 / D))
    for rows, mean in zip(blocks, means):
        total = jnp.zeros((32, 128), F32)
        for span in spans:
            centred = hidden[rows, span].astype(F32) - mean
            total = total + centred * centred
        scales.append(lax.rsqrt(jnp.sum(total, axis=1, keepdims=True) * (1.0 / D) + 1e-05))
    for rows, mean, scale in zip(blocks, means, scales):
        for span in spans:
            centred = hidden[rows, span].astype(F32) - mean
            hidden[rows, span] = (centred * scale * gain[:, span]).astype(BF16)


def front_kernel(
    codes, gain, hidden, probs, w_value, w_out, out_grad, err_out, err_value,
    mats_out, mats_value, left_out, own_half, other_half, gain_out, hidden_rows, gain_row,
    hidden_v, probs_v, w_value_v, w_value_t, w_out_v, grad_v, err_out_v, err_value_v,
    starts, values_t, d_mixed_t, mixed_t, d_values_t, mats_out_v, mats_value_v, left_sum, gain_v,
    codes_v, gain_flat, sems, out_sems, small_sems,
):
    half = TOK // 2
    halves = [pl.ds(part * half, half) for part in range(2)]
    pairs = (
        (hidden.at[halves[0]], hidden_v.at[halves[0]]),
        (w_out, w_out_v),
        (out_grad.at[halves[0]], grad_v.at[halves[0]]),
        (hidden.at[halves[1]], hidden_v.at[halves[1]]),
        (out_grad.at[halves[1]], grad_v.at[halves[1]]),
        (w_value, w_value_v),
        (probs, probs_v),
        (err_out.at[0], err_out_v),
        (err_value.at[0], err_value_v),
    )
    copies = [
        pltpu.make_async_copy(source, target, sems.at[index])
        for index, (source, target) in enumerate(pairs)
    ]
    small = (
        pltpu.make_async_copy(codes, codes_v, small_sems.at[0]),
        pltpu.make_async_copy(gain, gain_flat, small_sems.at[1]),
    )
    for copy in small:
        copy.start()
    for copy in copies[:4]:
        copy.start()
    index = lax.axis_index("tensor")
    rows_copy = pltpu.make_async_copy(
        hidden.at[pl.ds(pl.multiple_of(index * 128, 128), 128)], hidden_rows, out_sems.at[2 * STEPS]
    )

    def d_mixed_of(rows):
        d_mixed_t[:, rows] = dot(w_out_v[...], grad_v[rows, :], ((1,), (1,))).astype(BF16)

    for copy in small:
        copy.wait()
    @pl.loop(0, D // 128)
    def _(step):
        rows = pl.ds(pl.multiple_of(step * 128, 128), 128)
        for side in range(2):
            starts[side, rows, :] = start_rows(codes_v[side], step * 128, 128)

    for part in range(D // 128):
        span = pl.ds(part * 128, 128)
        gain_row[:, span] = gain_flat[span].reshape(1, 128)
    copies[0].wait()

    @pl.loop(0, half // LN_ROWS)
    def _(step):
        norm_rows(hidden_v, gain_row, step * LN_ROWS, LN_ROWS // 32)

    for copy in copies[4:6]:
        copy.start()
    for copy in copies[1:4]:
        copy.wait()
    for copy in copies[6:]:
        copy.start()
    rows_copy.start()

    @pl.loop(0, MERGE)
    def _(step):
        size = half // MERGE
        norm_rows(hidden_v, gain_row, half + step * size, size // 32)
        d_mixed_of(pl.ds(pl.multiple_of(step * size, size), size))

    for copy in copies[4:6]:
        copy.wait()

    @pl.loop(0, 2)
    def _(step):
        size = half // 2
        d_mixed_of(pl.ds(pl.multiple_of(half + step * size, size), size))
        for block in range(5):
            span = pl.ds(pl.multiple_of(step * 1280 + block * 256, 256), 256)
            w_value_t[:, span] = w_value_v[span, :].T

    for rows in halves:
        values_t[:, rows] = dot(w_value_t[...], hidden_v[rows, :], ((1,), (1,))).astype(BF16)

    copies[6].wait()
    for crop in range(CROPS):
        rows = pl.ds(crop * LEN, LEN)
        for head in range(HEADS_DEV):
            cols = pl.ds(head * HEAD_DIM, HEAD_DIM)
            weights = probs_v[crop, head]
            mixed_t[cols, rows] = dot(values_t[cols, rows], weights, ((1,), (1,))).astype(BF16)
            d_values_t[cols, rows] = dot(d_mixed_t[cols, rows], weights).astype(BF16)

    chip, core = place()
    for block in range(8):
        slot = pl.ds(pl.multiple_of(lax.rem(block // 2 - chip + 4, 4) * 128, 128), 128)
        part = d_values_t[:, pl.ds(block * 128, 128)]

        @pl.when(core == block % 2)
        def _():
            own_half[:, slot] = part

        @pl.when(core != block % 2)
        def _():
            other_half[:, slot] = part

    sides = (
        (copies[7], mixed_t, grad_v, err_out_v, mats_out_v, mats_out),
        (copies[8], d_values_t, hidden_v, err_value_v, mats_value_v, mats_value),
    )

    def write(index, step):
        span = pl.ds(step * TILE, TILE)
        mats_v, mats = sides[index][4:]
        return pltpu.make_async_copy(
            mats_v.at[:, span], mats.at[:, span], out_sems.at[index * STEPS + step]
        )

    for index, (copy, acts_t, other_side, err_v, mats_v, mats) in enumerate(sides):
        copy.wait()
        left_sum[...] = jnp.zeros((COLS, 128), F32)

        for step in range(STEPS):
            span = pl.ds(step * TILE, TILE)
            grad = dot(acts_t[...], other_side[:, span])
            rounded = (grad + err_v[:, span]).astype(BF16)
            mats_v[:, span] = rounded
            write(index, step).start()
            left_sum[...] += dot(rounded, starts[index, span, :])
            if index == 1:
                turned = w_value_t[:, span].astype(F32)
                gain_v[:, span] = jnp.sum(grad * turned, axis=0, keepdims=True) / gain_row[:, span]

        turned = left_sum[...].T
        left_out[pl.ds(index * RANK, RANK), :] = (
            turned[0:32] + (turned[32:64] + turned[64:96])
        ).astype(BF16)
    gain_out[...] = jnp.zeros((2 * RANK, 128), F32)
    for part in range(D // 128):
        gain_out[pl.ds(part // 3 * 8 + part % 3, 1), :] = gain_v[:, pl.ds(part * 128, 128)]

    for step in range(STEPS):
        for index in range(2):
            write(index, step).wait()
    rows_copy.wait()


def front(codes, gain, hidden, probs, w_value, w_out, out_grad, err_out, err_value):
    vmem = pl.BlockSpec(memory_space=pltpu.VMEM)
    return pl.pallas_call(
        front_kernel,
        name="front",
        out_shape=(
            jax.ShapeDtypeStruct((COLS, D), BF16),
            jax.ShapeDtypeStruct((COLS, D), BF16),
            jax.ShapeDtypeStruct((2 * RANK, COLS), BF16),
            jax.ShapeDtypeStruct((COLS, TOK // 2), BF16),
            jax.ShapeDtypeStruct((COLS, TOK // 2), BF16),
            jax.ShapeDtypeStruct((2 * RANK, 128), F32),
            jax.ShapeDtypeStruct((128, D), BF16),
            jax.ShapeDtypeStruct((1, D), F32),
        ),
        in_specs=[ANY] * 9,
        out_specs=(ANY, ANY, vmem, vmem, vmem, vmem, ANY, vmem),
        scratch_shapes=[
            pltpu.VMEM((TOK, D), BF16),
            pltpu.VMEM((CROPS, HEADS_DEV, LEN, LEN), BF16),
            pltpu.VMEM((D, COLS), BF16),
            pltpu.VMEM((COLS, D), BF16),
            pltpu.VMEM((COLS, D), BF16),
            pltpu.VMEM((TOK, D), BF16),
            pltpu.VMEM((COLS, D), F32),
            pltpu.VMEM((COLS, D), F32),
            pltpu.VMEM((2, D, 128), BF16),
            pltpu.VMEM((COLS, TOK), BF16),
            pltpu.VMEM((COLS, TOK), BF16),
            pltpu.VMEM((COLS, TOK), BF16),
            pltpu.VMEM((COLS, TOK), BF16),
            pltpu.VMEM((COLS, D), BF16),
            pltpu.VMEM((COLS, D), BF16),
            pltpu.VMEM((COLS, 128), F32),
            pltpu.VMEM((1, D), F32),
            pltpu.SMEM((2,), jnp.int32),
            pltpu.VMEM((D,), F32),
            pltpu.SemaphoreType.DMA((9,)),
            pltpu.SemaphoreType.DMA((2 * STEPS + 1,)),
            pltpu.SemaphoreType.DMA((2,)),
        ],
        compiler_params=pltpu.CompilerParams(vmem_limit_bytes=48 * 2**20),
        cost_estimate=pl.CostEstimate(
            flops=11 * 10**9, bytes_accessed=32 * 10**6, transcendentals=0
        ),
    )(
        pltpu.with_memory_space_constraint(codes, pltpu.HBM),
        pltpu.with_memory_space_constraint(gain, pltpu.HBM),
        hidden, probs, w_value, w_out, out_grad, err_out, err_value,
    )


def branch_kernel(
    own_half, other_half, w_own, w_other, here, after, before, far_after, far_before, d_values
):
    @pl.when(pl.program_id(0) == 0)
    def _():
        for block in range(2):
            rows = pl.ds(block * 256, 256)
            d_values[rows, pl.ds(0, COLS)] = own_half[:, rows].T
            d_values[rows, pl.ds(COLS, COLS)] = other_half[:, rows].T

    weights = jnp.concatenate([w_own[...], w_other[...]], axis=1)
    product = dot(d_values[...], weights, ((1,), (1,))).astype(BF16)
    here[...] = product[0:128]
    after[...] = product[128:256]
    far_after[...] = product[256:320]
    far_before[...] = product[320:384]
    before[...] = product[384:512]


def branch(own_half, other_half, w_own, w_other):
    half = pl.BlockSpec((COLS, TOK // 2), lambda n: (0, 0))
    weights = pl.BlockSpec((1280, COLS), lambda n: (n, 0))
    rows = (128, 128, 128, 64, 64)
    return pl.pallas_call(
        branch_kernel,
        name="branch",
        grid=(2,),
        out_shape=[jax.ShapeDtypeStruct((count, D), BF16) for count in rows],
        in_specs=[half, half, weights, weights],
        out_specs=[pl.BlockSpec((count, 1280), lambda n: (0, n)) for count in rows],
        scratch_shapes=[pltpu.VMEM((TOK // 2, 2 * COLS), BF16)],
        compiler_params=pltpu.CompilerParams(vmem_limit_bytes=20 * 2**20),
        cost_estimate=pl.CostEstimate(
            flops=2 * 10**9, bytes_accessed=7 * 10**6, transcendentals=0
        ),
    )(
        own_half,
        other_half,
        pltpu.with_memory_space_constraint(w_own, pltpu.HBM),
        w_other,
    )


def relay_kernel(after, before, far_after, far_before, next_after, next_before):
    top, low = pl.ds(0, 64), pl.ds(64, 64)
    next_after[top, :] = (after[top, :].astype(F32) + far_after[...].astype(F32)).astype(BF16)
    next_after[low, :] = after[low, :]
    next_before[top, :] = before[top, :]
    next_before[low, :] = (before[low, :].astype(F32) + far_before[...].astype(F32)).astype(BF16)


def relay(after, before, far_after, far_before):
    whole = pl.BlockSpec((128, 2560), lambda n: (0, n))
    part = pl.BlockSpec((64, 2560), lambda n: (0, n))
    return pl.pallas_call(
        relay_kernel,
        name="relay",
        grid=(1,),
        out_shape=(jax.ShapeDtypeStruct((128, D), BF16),) * 2,
        in_specs=[whole, whole, part, part],
        out_specs=(whole, whole),
        compiler_params=pltpu.CompilerParams(vmem_limit_bytes=8 * 2**20),
        cost_estimate=pl.CostEstimate(
            flops=10**6, bytes_accessed=4 * 10**6, transcendentals=0
        ),
    )(*(
        pltpu.with_memory_space_constraint(part, pltpu.HBM)
        for part in (after, before, far_after, far_before)
    ))


def norm_back_kernel(hidden, gain, here, after, before, in_grad, total, standard):
    spans = [pl.ds(part * 128, 128) for part in range(D // 128)]
    for block in range(4):
        rows = pl.ds(block * 32, 32)
        mean = jnp.zeros((32, 128), F32)
        for span in spans:
            mean = mean + hidden[rows, span].astype(F32)
        mean = jnp.sum(mean, axis=1, keepdims=True) * (1.0 / D)
        square = jnp.zeros((32, 128), F32)
        for span in spans:
            centred = hidden[rows, span].astype(F32) - mean
            square = square + centred * centred
        inv_std = lax.rsqrt(jnp.sum(square, axis=1, keepdims=True) * (1.0 / D) + 1e-05)
        first = jnp.zeros((32, 128), F32)
        second = jnp.zeros((32, 128), F32)
        for span in spans:
            summed = here[rows, span].astype(F32) + (
                after[rows, span].astype(F32) + before[rows, span].astype(F32)
            )
            scaled = summed * gain[:, span]
            unit = (hidden[rows, span].astype(F32) - mean) * inv_std
            total[rows, span] = scaled
            standard[rows, span] = unit
            first = first + scaled
            second = second + scaled * unit
        first = jnp.sum(first, axis=1, keepdims=True) * (1.0 / D)
        second = jnp.sum(second, axis=1, keepdims=True) * (1.0 / D)
        for span in spans:
            in_grad[rows, span] = (
                inv_std * (total[rows, span] - first - standard[rows, span] * second)
            ).astype(BF16)


def norm_back(hidden, gain, here, after, before):
    rows = pl.BlockSpec((128, D), lambda n: (n, 0))
    return pl.pallas_call(
        norm_back_kernel,
        name="norm_back",
        grid=(1,),
        in_specs=[rows, pl.BlockSpec((1, D), lambda n: (0, 0)), rows, rows, rows],
        out_specs=rows,
        scratch_shapes=[pltpu.VMEM((128, D), F32), pltpu.VMEM((128, D), F32)],
        out_shape=jax.ShapeDtypeStruct((128, D), BF16),
        compiler_params=pltpu.CompilerParams(vmem_limit_bytes=16 * 2**20),
        cost_estimate=pl.CostEstimate(
            flops=5 * 10**6, bytes_accessed=10**6, transcendentals=0
        ),
    )(hidden, gain, here, after, before)


def right_kernel(left, gain_rows, mats_out, mats_value, own, other, staged):
    chip, core = place()
    step = pl.program_id(0)
    lanes = pl.ds(pl.multiple_of(step * 2560, 2560), 2560)

    def put(side, span, value):
        for block in range(4):
            rows = pl.ds(pl.multiple_of(lax.rem(block - chip + 4, 4) * 8, 8), 8)
            part = value[block * 8 : (block + 1) * 8]

            @pl.when(core == side)
            def _():
                own[rows, span] = part

            @pl.when(core != side)
            def _():
                staged[rows, span] = part

    for side, mats in enumerate((mats_out, mats_value)):
        span = pl.ds(side * RANK, RANK)
        rows = left[span, :]
        parts = jnp.concatenate(split2(rows), axis=0)
        product = dot(parts, mats[...])
        put(side, lanes, product[:RANK] + product[RANK:])

        @pl.when(step == 0)
        def _():
            gram = dot_split(rows, rows, ((1,), (1,)))
            packed = jnp.concatenate([gram[8 * k : 8 * k + 8] for k in range(4)], axis=1)
            put(side, pl.ds(D, 128), gain_rows[span, :])
            high, low = split2(packed)
            for place_at, part in ((SENT, high), (SENT + 128, low)):
                put(side, pl.ds(place_at, 128), jnp.concatenate([part.astype(F32)] * 4, axis=0))

    @pl.when(step == 0)
    def _():
        other[...] = staged[...].astype(BF16)


def right_terms(left, gain_rows, mats_out, mats_value):
    whole = pl.BlockSpec((RANK, WIDE), lambda n: (0, 0))
    mats = pl.BlockSpec((COLS, 2560), lambda n: (0, n))
    return pl.pallas_call(
        right_kernel,
        name="right_terms",
        grid=(1,),
        out_shape=(
            jax.ShapeDtypeStruct((RANK, WIDE), F32),
            jax.ShapeDtypeStruct((RANK, WIDE), BF16),
        ),
        in_specs=[
            pl.BlockSpec((2 * RANK, COLS), lambda n: (0, 0)),
            pl.BlockSpec((2 * RANK, 128), lambda n: (0, 0)),
            mats,
            mats,
        ],
        out_specs=(whole, whole),
        scratch_shapes=[pltpu.VMEM((RANK, WIDE), F32)],
        compiler_params=pltpu.CompilerParams(vmem_limit_bytes=16 * 2**20),
        cost_estimate=pl.CostEstimate(
            flops=5 * 10**8, bytes_accessed=5 * 10**6, transcendentals=0
        ),
    )(left, gain_rows, mats_out, mats_value)


def merge_kernel(ours, theirs, own, to_opposite, to_after, to_before):
    total = ours[...] + theirs[...].astype(F32)
    gram = total[:8, SENT : SENT + 128] + total[:8, SENT + 128 :]
    grams = split2(gram)
    own[:, pl.ds(0, SENT)] = total[:8, :SENT]
    own[:, pl.ds(SENT, 128)] = gram
    for slot, target in ((1, to_after), (2, to_opposite), (3, to_before)):
        target[:, pl.ds(0, SENT)] = total[8 * slot : 8 * slot + 8, :SENT].astype(BF16)
        for part, value in enumerate(grams):
            target[:, pl.ds(SENT + 128 * part, 128)] = value


def merge(ours, theirs):
    return pl.pallas_call(
        merge_kernel,
        name="merge",
        out_shape=(
            jax.ShapeDtypeStruct((8, SENT + 128), F32),
            *[jax.ShapeDtypeStruct((8, WIDE), BF16) for _ in range(3)],
        ),
        compiler_params=pltpu.CompilerParams(vmem_limit_bytes=8 * 2**20),
        cost_estimate=pl.CostEstimate(
            flops=10**5, bytes_accessed=7 * 10**5, transcendentals=0
        ),
    )(ours, theirs)


def collect_kernel(own, opposite, after, before, chunk, gram):
    parts = [part[...].astype(F32) for part in (opposite, after, before)]
    total = (own[:, pl.ds(0, SENT)] + parts[0][:, :SENT]) + (
        parts[1][:, :SENT] + parts[2][:, :SENT]
    )
    chunk[...] = total.astype(BF16)
    parts = [part[:, SENT : SENT + 128] + part[:, SENT + 128 :] for part in parts]
    packed = (own[:, pl.ds(SENT, 128)] + parts[0]) + (parts[1] + parts[2])
    square = jnp.concatenate([packed[:, k * RANK : (k + 1) * RANK] for k in range(4)], axis=0)
    wide = jnp.concatenate([square, jnp.zeros((RANK, 128 - RANK), F32)], axis=1)
    for part, value in enumerate(split2(wide)):
        gram[:, pl.ds(part * 128, 128)] = value


def collect(own, opposite, after, before):
    return pl.pallas_call(
        collect_kernel,
        name="collect",
        out_shape=(
            jax.ShapeDtypeStruct((8, SENT), BF16),
            jax.ShapeDtypeStruct((RANK, 256), BF16),
        ),
        compiler_params=pltpu.CompilerParams(vmem_limit_bytes=8 * 2**20),
        cost_estimate=pl.CostEstimate(
            flops=10**5, bytes_accessed=3 * 10**5, transcendentals=0
        ),
    )(own, opposite, after, before)


def factor_kernel(parts, inverse):
    gram = parts[:, pl.ds(0, 128)].astype(F32) + parts[:, pl.ds(128, 128)].astype(F32)
    row_ids = lax.broadcasted_iota(jnp.int32, (RANK, 128), 0)
    col_ids = lax.broadcasted_iota(jnp.int32, (RANK, 128), 1)
    unit = jnp.where(row_ids + RANK == col_ids, 1.0, 0.0)
    work = unit + gram
    for step in range(0, RANK, 2):
        first, second = work[step : step + 1, :], work[step + 1 : step + 2, :]
        column = jnp.broadcast_to(work[:, step : step + 1], (RANK, 128))
        other = jnp.broadcast_to(work[:, step + 1 : step + 2], (RANK, 128))
        scale = 1.0 / column[step : step + 1, :]
        ratio = other[step : step + 1, :] * scale
        other = other - column * ratio
        second = second - first * ratio
        after = row_ids > step + 1
        work = jnp.where(row_ids == step + 1, second, work) - jnp.where(
            after,
            column * (first * scale) + other * (second / other[step + 1 : step + 2, :]),
            0.0,
        )
    diagonal = jnp.sum(jnp.where(row_ids == col_ids, work, 0.0), axis=1, keepdims=True)
    scaled = work * lax.rsqrt(diagonal)
    high, low = split2(pltpu.roll(scaled, 128 - RANK, 1))
    inverse[:, pl.ds(0, 128)] = high
    inverse[:, pl.ds(128, 128)] = low


def factor(parts):
    return pl.pallas_call(
        factor_kernel,
        name="factor",
        out_shape=jax.ShapeDtypeStruct((RANK, 256), BF16),
        cost_estimate=pl.CostEstimate(
            flops=5 * 10**6, bytes_accessed=3 * 10**6, transcendentals=0
        ),
    )(parts)


def finish_kernel(
    ours, theirs, left, mats_out, mats_value,
    err_out, err_value, share_out, share_value, ortho_out, ortho_value, gain_out,
    sums, ortho_parts, right,
):
    chip, core = place()
    step = pl.program_id(0)
    lanes = pl.ds(pl.multiple_of(step * 1280, 1280), 1280)

    @pl.when(step == 0)
    def _():
        for side, source in ((core, ours), (1 - core, theirs)):
            wide = source[...].astype(F32)
            for block in range(4):
                offset = lax.rem(chip + block, 4) * 8
                rows = pl.ds(pl.multiple_of(side * RANK + offset, 8), 8)
                sums[rows, pl.ds(0, SENT)] = wide[block * 8 : block * 8 + 8, :SENT]
            rows = pl.ds(pl.multiple_of(side * RANK, RANK), RANK)
            sums[rows, pl.ds(SENT, 128)] = wide[:, SENT : SENT + 128] + wide[:, SENT + 128 :]
        for part in range(D // 128):
            row = sums[pl.ds(part // 3 * 8 + part % 3, 1), pl.ds(D, 128)]
            gain_out[pl.ds(part * 128, 128)] = row.reshape(128)
        for side, scaled in enumerate((ortho_out, ortho_value)):
            span = pl.ds(side * RANK, RANK)
            inverse = sums[span, pl.ds(SENT, 128)][:, :RANK]
            ortho = dot_split(inverse, left[span, :])
            scaled[...] = ortho * math.sqrt(HH)
            high, low = split2(ortho)
            parts = jnp.concatenate([high, low, high, jnp.zeros_like(high)], axis=0)
            ortho_parts[side] = parts.T

    for side, (mats, err) in enumerate(((mats_out, err_out), (mats_value, err_value))):
        span = pl.ds(side * RANK, RANK)
        inverse = sums[span, pl.ds(SENT, 128)][:, :RANK]
        rows = dot_split(inverse, sums[span, lanes]) * (1.0 / WORKERS)
        right[span, lanes] = rows
        high, low = split2(rows)
        parts = jnp.concatenate([high, high, low, jnp.zeros_like(high)], axis=0)
        err[0] = mats[...].astype(F32) - dot(ortho_parts[side], parts)

    @pl.when(step == 1)
    def _():
        index = chip * 2 + core
        window = right[:, pl.ds(pl.multiple_of(index * 5 // 2 * 128, 128), 512)]
        window = jnp.where(lax.rem(index, 2) == 1, pltpu.roll(window, 512 - 64, 1), window)
        share_out[...] = window[:RANK, : D // 8]
        share_value[...] = window[RANK:, : D // 8]


def finish(ours, theirs, left, mats_out, mats_value):
    whole = pl.BlockSpec((RANK, WIDE), lambda n: (0, 0))
    mats = pl.BlockSpec((COLS, 1280), lambda n: (0, n))
    err = pl.BlockSpec((1, COLS, 1280), lambda n: (0, 0, n))
    share = pl.BlockSpec((RANK, D // 8), lambda n: (0, 0))
    ortho = pl.BlockSpec((RANK, COLS), lambda n: (0, 0))
    return pl.pallas_call(
        finish_kernel,
        name="finish",
        grid=(2,),
        out_shape=(
            jax.ShapeDtypeStruct((1, COLS, D), F32),
            jax.ShapeDtypeStruct((1, COLS, D), F32),
            jax.ShapeDtypeStruct((RANK, D // 8), F32),
            jax.ShapeDtypeStruct((RANK, D // 8), F32),
            jax.ShapeDtypeStruct((RANK, COLS), F32),
            jax.ShapeDtypeStruct((RANK, COLS), F32),
            jax.ShapeDtypeStruct((D,), F32),
        ),
        in_specs=[
            whole, whole, pl.BlockSpec((2 * RANK, COLS), lambda n: (0, 0)), mats, mats,
        ],
        out_specs=(
            err, err, share, share, ortho, ortho, pl.BlockSpec((D,), lambda n: (0,)),
        ),
        scratch_shapes=[
            pltpu.VMEM((2 * RANK, WIDE), F32),
            pltpu.VMEM((2, COLS, 4 * RANK), BF16),
            pltpu.VMEM((2 * RANK, WIDE), F32),
        ],
        compiler_params=pltpu.CompilerParams(vmem_limit_bytes=20 * 2**20),
        cost_estimate=pl.CostEstimate(
            flops=1 * 10**9, bytes_accessed=13 * 10**6, transcendentals=0
        ),
    )(ours, theirs, left, mats_out, mats_value)


def to_core(value):
    return lax.ppermute(value, "tensor", [(i, i ^ 1) for i in range(8)])


def to_x(value, hops):
    return lax.ppermute(value, "tensor", [(i, (i // 2 + hops) % 4 * 2 + i % 2) for i in range(8)])


def to_z(value, hops):
    return lax.ppermute(value, "dp", [(i, i // 4 * 4 + (i + hops) % 4) for i in range(16)])


def to_y(value, hops):
    return lax.ppermute(value, "dp", [(i, (i // 4 + hops) % 4 * 4 + i % 4) for i in range(16)])


def rounded(value):
    return lax.reduce_precision(value, 8, 7).astype(BF16)


def ring_sum(value, send, beside=()):
    parts = send(value, 2), send(value, 1), send(value, 3)
    parts, beside = lax.optimization_barrier((parts, beside))
    opposite, after, before = (part.astype(F32) for part in parts)
    total = (value.astype(F32) + opposite) + (after + before)
    return (total, *beside) if beside else total


def local(
    hidden_in, ln_gain, attn_probs, w_value, w_out, out_grad, err_out, err_value, factor_codes
):
    w_other = to_core(w_value)
    (
        mats_out, mats_value, left_term, own_half, other_half, gain_rows, hidden_rows, gain_row
    ) = front(
        factor_codes, ln_gain, hidden_in, attn_probs, w_value, w_out, out_grad,
        err_out, err_value,
    )
    received_half = to_core(other_half)

    here, after, before, far_after, far_before = branch(own_half, received_half, w_value, w_other)
    left, far_after, far_before = ring_sum(left_term, to_z, (far_after, far_before))
    far_after, far_before = to_x(far_after, 1), to_x(far_before, 3)
    left, far_after, far_before = ring_sum(rounded(left), to_y, (far_after, far_before))

    ours, theirs = right_terms(left, gain_rows, mats_out, mats_value)
    own, to_opposite, to_after, to_before = merge(ours, to_core(theirs))
    next_after, next_before = relay(after, before, far_after, far_before)
    parts = to_x(to_opposite, 2), to_x(to_after, 1), to_x(to_before, 3)
    parts, next_after, next_before = lax.optimization_barrier((parts, next_after, next_before))
    chunk, gram = collect(own, *parts)
    chunk, gram, next_after, next_before = lax.optimization_barrier(
        (chunk, gram, next_after, next_before)
    )
    near_after, near_before = to_x(next_after, 1), to_x(next_before, 3)

    def over_workers(step, carry):
        chunk, inverse = ring_sum(carry[0], to_z, (factor(carry[1]),))
        return rounded(ring_sum(rounded(chunk), to_y)), inverse

    passes = 1 + lax.axis_index("dp") // WORKERS
    chunk, inverse = lax.fori_loop(0, passes, over_workers, (chunk, gram))
    chunk, near_after, near_before = lax.optimization_barrier((chunk, near_after, near_before))
    in_grad = norm_back(hidden_rows, gain_row, here, near_after, near_before)
    parts = to_x(chunk, 2), to_x(chunk, 3), to_x(chunk, 1)
    (opposite, after, before), in_grad = lax.optimization_barrier((parts, in_grad))
    rows = jnp.concatenate([chunk, after, opposite, before], axis=0)
    ours = jnp.concatenate([rows, inverse], axis=1)
    theirs = to_core(ours)
    new_out, new_value, share_out, share_value, ortho_out, ortho_value, gain_grad = finish(
        ours, theirs, left, mats_out, mats_value
    )
    return (
        in_grad,
        gain_grad,
        new_out,
        new_value,
        ortho_out.T,
        ortho_value.T,
        share_out.T,
        share_value.T,
    )


def solution(mesh):
    in_specs = (
        P("dp", None),
        P(),
        P("dp", "tensor", None, None),
        P(None, "tensor"),
        P("tensor", None),
        P("dp", None),
        P("dp", "tensor", None),
        P("dp", "tensor", None),
        P(),
    )
    out_specs = (
        P(("dp", "tensor"), None),
        P(),
        P("dp", "tensor", None),
        P("dp", "tensor", None),
        P("tensor", None),
        P("tensor", None),
        P("tensor", None),
        P("tensor", None),
    )
    return jax.shard_map(local, mesh=mesh, in_specs=in_specs, out_specs=out_specs, check_vma=False)
```

```python
import math

import jax
import jax.numpy as jnp
from jax import lax
from jax.experimental import pallas as pl
from jax.experimental.pallas import tpu as pltpu
from jax.sharding import PartitionSpec as P

D = 2560
RANK = 32
HEADS = 24
HEAD_DIM = 128
LEN = 512
CROPS = 2
HEADS_DEV = 3
TOK = CROPS * LEN
COLS = HEADS_DEV * HEAD_DIM
HH = HEADS * HEAD_DIM
SENT = D + 128
WIDE = D + 384
TILE = 512
STEPS = D // TILE
LN_ROWS = 512
MERGE = 2
WORKERS = 16
F32 = jnp.float32
BF16 = jnp.bfloat16
ANY = pl.BlockSpec(memory_space=pl.ANY)
SMEM = pl.BlockSpec(memory_space=pltpu.SMEM)


def place():
    index = lax.axis_index("tensor")
    return lax.div(index, 2), lax.rem(index, 2)


def dot(a, b, dims=((1,), (0,))):
    return lax.dot_general(a, b, (dims, ((), ())), preferred_element_type=F32)


def split2(a):
    high = a.astype(BF16)
    return high, (a - high.astype(F32)).astype(BF16)


def dot_split(a, b, dims=((1,), (0,))):
    a_high, a_low = split2(a)
    b_high, b_low = split2(b)
    return dot(a_high, b_high, dims) + (dot(a_low, b_high, dims) + dot(a_high, b_low, dims))


def lane_parts(value, group):
    high = value.astype(BF16).astype(F32)
    rest = value - high
    middle = rest.astype(BF16).astype(F32)
    low = rest - middle
    zero = jnp.zeros_like(value)
    return jnp.where(
        group == 0, high, jnp.where(group == 1, middle, jnp.where(group == 2, low, zero))
    ).astype(BF16)


def start_rows(code, first, rows):
    row_ids = lax.broadcasted_iota(jnp.int32, (rows, 128), 0) + first
    lane = lax.broadcasted_iota(jnp.int32, (rows, 128), 1)
    hashed = row_ids * 40503 + jnp.bitwise_and(lane, RANK - 1) * 1531 + code * 7919
    hashed = jnp.bitwise_xor(hashed, jnp.right_shift(hashed, 15)) * 668265261
    hashed = jnp.bitwise_xor(hashed, jnp.right_shift(hashed, 15)) * 374761393
    hashed = jnp.bitwise_xor(hashed, jnp.right_shift(hashed, 13))
    level = jnp.bitwise_and(hashed, 8388607).astype(F32)
    start = ((level + 0.5) / 8388608.0 - 0.5) * math.sqrt(12.0)
    return lane_parts(start, jnp.right_shift(lane, 5))


def norm_rows(hidden, gain, first, count):
    blocks = [pl.ds(pl.multiple_of(first + 32 * block, 32), 32) for block in range(count)]
    spans = [pl.ds(part * 128, 128) for part in range(D // 128)]
    means, scales = [], []
    for rows in blocks:
        total = hidden[rows, spans[0]].astype(F32)
        for span in spans[1:]:
            total = total + hidden[rows, span].astype(F32)
        means.append(jnp.sum(total, axis=1, keepdims=True) * (1.0 / D))
    for rows, mean in zip(blocks, means):
        total = jnp.zeros((32, 128), F32)
        for span in spans:
            centred = hidden[rows, span].astype(F32) - mean
            total = total + centred * centred
        scales.append(lax.rsqrt(jnp.sum(total, axis=1, keepdims=True) * (1.0 / D) + 1e-05))
    for rows, mean, scale in zip(blocks, means, scales):
        for span in spans:
            centred = hidden[rows, span].astype(F32) - mean
            hidden[rows, span] = (centred * scale * gain[:, span]).astype(BF16)


def front_kernel(
    codes, gain, hidden, probs, w_value, w_out, out_grad, err_out, err_value,
    mats_out, mats_value, left_out, own_half, other_half, gain_out, hidden_rows, gain_row,
    hidden_v, probs_v, w_value_v, w_value_t, w_out_v, grad_v, err_out_v, err_value_v,
    starts, values_t, d_mixed_t, mixed_t, d_values_t, mats_out_v, mats_value_v, left_sum, gain_v,
    codes_v, gain_flat, sems, out_sems, small_sems,
):
    half = TOK // 2
    halves = [pl.ds(part * half, half) for part in range(2)]
    pairs = (
        (hidden.at[halves[0]], hidden_v.at[halves[0]]),
        (w_out, w_out_v),
        (out_grad.at[halves[0]], grad_v.at[halves[0]]),
        (hidden.at[halves[1]], hidden_v.at[halves[1]]),
        (out_grad.at[halves[1]], grad_v.at[halves[1]]),
        (w_value, w_value_v),
        (probs, probs_v),
        (err_out.at[0], err_out_v),
        (err_value.at[0], err_value_v),
    )
    copies = [
        pltpu.make_async_copy(source, target, sems.at[index])
        for index, (source, target) in enumerate(pairs)
    ]
    small = (
        pltpu.make_async_copy(codes, codes_v, small_sems.at[0]),
        pltpu.make_async_copy(gain, gain_flat, small_sems.at[1]),
    )
    for copy in small:
        copy.start()
    for copy in copies[:2]:
        copy.start()
    index = lax.axis_index("tensor")
    rows_copy = pltpu.make_async_copy(
        hidden.at[pl.ds(pl.multiple_of(index * 128, 128), 128)], hidden_rows, out_sems.at[2 * STEPS]
    )

    def d_mixed_of(rows):
        d_mixed_t[:, rows] = dot(w_out_v[...], grad_v[rows, :], ((1,), (1,))).astype(BF16)

    for copy in small:
        copy.wait()
    @pl.loop(0, D // 128)
    def _(step):
        rows = pl.ds(pl.multiple_of(step * 128, 128), 128)
        for side in range(2):
            starts[side, rows, :] = start_rows(codes_v[side], step * 128, 128)

    for part in range(D // 128):
        span = pl.ds(part * 128, 128)
        gain_row[:, span] = gain_flat[span].reshape(1, 128)
    copies[0].wait()
    for copy in copies[2:4]:
        copy.start()

    @pl.loop(0, half // LN_ROWS)
    def _(step):
        norm_rows(hidden_v, gain_row, step * LN_ROWS, LN_ROWS // 32)

    for copy in copies[4:6]:
        copy.start()
    for copy in copies[1:4]:
        copy.wait()
    for copy in copies[6:]:
        copy.start()
    rows_copy.start()

    @pl.loop(0, MERGE)
    def _(step):
        size = half // MERGE
        norm_rows(hidden_v, gain_row, half + step * size, size // 32)
        d_mixed_of(pl.ds(pl.multiple_of(step * size, size), size))

    for copy in copies[4:6]:
        copy.wait()

    @pl.loop(0, 2)
    def _(step):
        size = half // 2
        d_mixed_of(pl.ds(pl.multiple_of(half + step * size, size), size))
        for block in range(5):
            span = pl.ds(pl.multiple_of(step * 1280 + block * 256, 256), 256)
            w_value_t[:, span] = w_value_v[span, :].T

    for rows in halves:
        values_t[:, rows] = dot(w_value_t[...], hidden_v[rows, :], ((1,), (1,))).astype(BF16)

    copies[6].wait()
    for crop in range(CROPS):
        rows = pl.ds(crop * LEN, LEN)
        for head in range(HEADS_DEV):
            cols = pl.ds(head * HEAD_DIM, HEAD_DIM)
            weights = probs_v[crop, head]
            mixed_t[cols, rows] = dot(values_t[cols, rows], weights, ((1,), (1,))).astype(BF16)
            d_values_t[cols, rows] = dot(d_mixed_t[cols, rows], weights).astype(BF16)

    chip, core = place()
    for block in range(8):
        slot = pl.ds(pl.multiple_of(lax.rem(block // 2 - chip + 4, 4) * 128, 128), 128)
        part = d_values_t[:, pl.ds(block * 128, 128)]

        @pl.when(core == block % 2)
        def _():
            own_half[:, slot] = part

        @pl.when(core != block % 2)
        def _():
            other_half[:, slot] = part

    sides = (
        (copies[7], mixed_t, grad_v, err_out_v, mats_out_v, mats_out),
        (copies[8], d_values_t, hidden_v, err_value_v, mats_value_v, mats_value),
    )

    def write(index, step):
        span = pl.ds(step * TILE, TILE)
        mats_v, mats = sides[index][4:]
        return pltpu.make_async_copy(
            mats_v.at[:, span], mats.at[:, span], out_sems.at[index * STEPS + step]
        )

    for index, (copy, acts_t, other_side, err_v, mats_v, mats) in enumerate(sides):
        copy.wait()
        left_sum[...] = jnp.zeros((COLS, 128), F32)

        for step in range(STEPS):
            span = pl.ds(step * TILE, TILE)
            grad = dot(acts_t[...], other_side[:, span])
            rounded = (grad + err_v[:, span]).astype(BF16)
            mats_v[:, span] = rounded
            write(index, step).start()
            left_sum[...] += dot(rounded, starts[index, span, :])
            if index == 1:
                turned = w_value_t[:, span].astype(F32)
                gain_v[:, span] = jnp.sum(grad * turned, axis=0, keepdims=True) / gain_row[:, span]

        turned = left_sum[...].T
        left_out[pl.ds(index * RANK, RANK), :] = (
            turned[0:32] + (turned[32:64] + turned[64:96])
        ).astype(BF16)
    gain_out[...] = jnp.zeros((2 * RANK, 128), F32)
    for part in range(D // 128):
        gain_out[pl.ds(part // 3 * 8 + part % 3, 1), :] = gain_v[:, pl.ds(part * 128, 128)]

    for step in range(STEPS):
        for index in range(2):
            write(index, step).wait()
    rows_copy.wait()


def front(codes, gain, hidden, probs, w_value, w_out, out_grad, err_out, err_value):
    vmem = pl.BlockSpec(memory_space=pltpu.VMEM)
    return pl.pallas_call(
        front_kernel,
        name="front",
        out_shape=(
            jax.ShapeDtypeStruct((COLS, D), BF16),
            jax.ShapeDtypeStruct((COLS, D), BF16),
            jax.ShapeDtypeStruct((2 * RANK, COLS), BF16),
            jax.ShapeDtypeStruct((COLS, TOK // 2), BF16),
            jax.ShapeDtypeStruct((COLS, TOK // 2), BF16),
            jax.ShapeDtypeStruct((2 * RANK, 128), F32),
            jax.ShapeDtypeStruct((128, D), BF16),
            jax.ShapeDtypeStruct((1, D), F32),
        ),
        in_specs=[ANY] * 9,
        out_specs=(ANY, ANY, vmem, vmem, vmem, vmem, ANY, vmem),
        scratch_shapes=[
            pltpu.VMEM((TOK, D), BF16),
            pltpu.VMEM((CROPS, HEADS_DEV, LEN, LEN), BF16),
            pltpu.VMEM((D, COLS), BF16),
            pltpu.VMEM((COLS, D), BF16),
            pltpu.VMEM((COLS, D), BF16),
            pltpu.VMEM((TOK, D), BF16),
            pltpu.VMEM((COLS, D), F32),
            pltpu.VMEM((COLS, D), F32),
            pltpu.VMEM((2, D, 128), BF16),
            pltpu.VMEM((COLS, TOK), BF16),
            pltpu.VMEM((COLS, TOK), BF16),
            pltpu.VMEM((COLS, TOK), BF16),
            pltpu.VMEM((COLS, TOK), BF16),
            pltpu.VMEM((COLS, D), BF16),
            pltpu.VMEM((COLS, D), BF16),
            pltpu.VMEM((COLS, 128), F32),
            pltpu.VMEM((1, D), F32),
            pltpu.SMEM((2,), jnp.int32),
            pltpu.VMEM((D,), F32),
            pltpu.SemaphoreType.DMA((9,)),
            pltpu.SemaphoreType.DMA((2 * STEPS + 1,)),
            pltpu.SemaphoreType.DMA((2,)),
        ],
        compiler_params=pltpu.CompilerParams(vmem_limit_bytes=48 * 2**20),
        cost_estimate=pl.CostEstimate(
            flops=11 * 10**9, bytes_accessed=32 * 10**6, transcendentals=0
        ),
    )(
        pltpu.with_memory_space_constraint(codes, pltpu.HBM),
        pltpu.with_memory_space_constraint(gain, pltpu.HBM),
        hidden, probs, w_value, w_out, out_grad, err_out, err_value,
    )


def branch_kernel(
    own_half, other_half, w_own, w_other, here, after, before, far_after, far_before, d_values
):
    @pl.when(pl.program_id(0) == 0)
    def _():
        for block in range(2):
            rows = pl.ds(block * 256, 256)
            d_values[rows, pl.ds(0, COLS)] = own_half[:, rows].T
            d_values[rows, pl.ds(COLS, COLS)] = other_half[:, rows].T

    weights = jnp.concatenate([w_own[...], w_other[...]], axis=1)
    product = dot(d_values[...], weights, ((1,), (1,))).astype(BF16)
    here[...] = product[0:128]
    after[...] = product[128:256]
    far_after[...] = product[256:320]
    far_before[...] = product[320:384]
    before[...] = product[384:512]


def branch(own_half, other_half, w_own, w_other):
    half = pl.BlockSpec((COLS, TOK // 2), lambda n: (0, 0))
    weights = pl.BlockSpec((1280, COLS), lambda n: (n, 0))
    rows = (128, 128, 128, 64, 64)
    return pl.pallas_call(
        branch_kernel,
        name="branch",
        grid=(2,),
        out_shape=[jax.ShapeDtypeStruct((count, D), BF16) for count in rows],
        in_specs=[half, half, weights, weights],
        out_specs=[pl.BlockSpec((count, 1280), lambda n: (0, n)) for count in rows],
        scratch_shapes=[pltpu.VMEM((TOK // 2, 2 * COLS), BF16)],
        compiler_params=pltpu.CompilerParams(vmem_limit_bytes=20 * 2**20),
        cost_estimate=pl.CostEstimate(
            flops=2 * 10**9, bytes_accessed=7 * 10**6, transcendentals=0
        ),
    )(
        own_half,
        other_half,
        pltpu.with_memory_space_constraint(w_own, pltpu.HBM),
        w_other,
    )


def relay_kernel(after, before, far_after, far_before, next_after, next_before):
    top, low = pl.ds(0, 64), pl.ds(64, 64)
    next_after[top, :] = (after[top, :].astype(F32) + far_after[...].astype(F32)).astype(BF16)
    next_after[low, :] = after[low, :]
    next_before[top, :] = before[top, :]
    next_before[low, :] = (before[low, :].astype(F32) + far_before[...].astype(F32)).astype(BF16)


def relay(after, before, far_after, far_before):
    whole = pl.BlockSpec((128, 2560), lambda n: (0, n))
    part = pl.BlockSpec((64, 2560), lambda n: (0, n))
    return pl.pallas_call(
        relay_kernel,
        name="relay",
        grid=(1,),
        out_shape=(jax.ShapeDtypeStruct((128, D), BF16),) * 2,
        in_specs=[whole, whole, part, part],
        out_specs=(whole, whole),
        compiler_params=pltpu.CompilerParams(vmem_limit_bytes=8 * 2**20),
        cost_estimate=pl.CostEstimate(
            flops=10**6, bytes_accessed=4 * 10**6, transcendentals=0
        ),
    )(*(
        pltpu.with_memory_space_constraint(part, pltpu.HBM)
        for part in (after, before, far_after, far_before)
    ))


def norm_back_kernel(hidden, gain, here, after, before, in_grad, total, standard):
    spans = [pl.ds(part * 128, 128) for part in range(D // 128)]
    for block in range(4):
        rows = pl.ds(block * 32, 32)
        mean = jnp.zeros((32, 128), F32)
        for span in spans:
            mean = mean + hidden[rows, span].astype(F32)
        mean = jnp.sum(mean, axis=1, keepdims=True) * (1.0 / D)
        square = jnp.zeros((32, 128), F32)
        for span in spans:
            centred = hidden[rows, span].astype(F32) - mean
            square = square + centred * centred
        inv_std = lax.rsqrt(jnp.sum(square, axis=1, keepdims=True) * (1.0 / D) + 1e-05)
        first = jnp.zeros((32, 128), F32)
        second = jnp.zeros((32, 128), F32)
        for span in spans:
            summed = here[rows, span].astype(F32) + (
                after[rows, span].astype(F32) + before[rows, span].astype(F32)
            )
            scaled = summed * gain[:, span]
            unit = (hidden[rows, span].astype(F32) - mean) * inv_std
            total[rows, span] = scaled
            standard[rows, span] = unit
            first = first + scaled
            second = second + scaled * unit
        first = jnp.sum(first, axis=1, keepdims=True) * (1.0 / D)
        second = jnp.sum(second, axis=1, keepdims=True) * (1.0 / D)
        for span in spans:
            in_grad[rows, span] = (
                inv_std * (total[rows, span] - first - standard[rows, span] * second)
            ).astype(BF16)


def norm_back(hidden, gain, here, after, before):
    rows = pl.BlockSpec((128, D), lambda n: (n, 0))
    return pl.pallas_call(
        norm_back_kernel,
        name="norm_back",
        grid=(1,),
        in_specs=[rows, pl.BlockSpec((1, D), lambda n: (0, 0)), rows, rows, rows],
        out_specs=rows,
        scratch_shapes=[pltpu.VMEM((128, D), F32), pltpu.VMEM((128, D), F32)],
        out_shape=jax.ShapeDtypeStruct((128, D), BF16),
        compiler_params=pltpu.CompilerParams(vmem_limit_bytes=16 * 2**20),
        cost_estimate=pl.CostEstimate(
            flops=5 * 10**6, bytes_accessed=10**6, transcendentals=0
        ),
    )(hidden, gain, here, after, before)


def right_kernel(left, gain_rows, mats_out, mats_value, own, other, staged):
    chip, core = place()
    step = pl.program_id(0)
    lanes = pl.ds(pl.multiple_of(step * 2560, 2560), 2560)

    def put(side, span, value):
        for block in range(4):
            rows = pl.ds(pl.multiple_of(lax.rem(block - chip + 4, 4) * 8, 8), 8)
            part = value[block * 8 : (block + 1) * 8]

            @pl.when(core == side)
            def _():
                own[rows, span] = part

            @pl.when(core != side)
            def _():
                staged[rows, span] = part

    for side, mats in enumerate((mats_out, mats_value)):
        span = pl.ds(side * RANK, RANK)
        rows = left[span, :]
        parts = jnp.concatenate(split2(rows), axis=0)
        product = dot(parts, mats[...])
        put(side, lanes, product[:RANK] + product[RANK:])

        @pl.when(step == 0)
        def _():
            gram = dot_split(rows, rows, ((1,), (1,)))
            packed = jnp.concatenate([gram[8 * k : 8 * k + 8] for k in range(4)], axis=1)
            put(side, pl.ds(D, 128), gain_rows[span, :])
            high, low = split2(packed)
            for place_at, part in ((SENT, high), (SENT + 128, low)):
                put(side, pl.ds(place_at, 128), jnp.concatenate([part.astype(F32)] * 4, axis=0))

    @pl.when(step == 0)
    def _():
        other[...] = staged[...].astype(BF16)


def right_terms(left, gain_rows, mats_out, mats_value):
    whole = pl.BlockSpec((RANK, WIDE), lambda n: (0, 0))
    mats = pl.BlockSpec((COLS, 2560), lambda n: (0, n))
    return pl.pallas_call(
        right_kernel,
        name="right_terms",
        grid=(1,),
        out_shape=(
            jax.ShapeDtypeStruct((RANK, WIDE), F32),
            jax.ShapeDtypeStruct((RANK, WIDE), BF16),
        ),
        in_specs=[
            pl.BlockSpec((2 * RANK, COLS), lambda n: (0, 0)),
            pl.BlockSpec((2 * RANK, 128), lambda n: (0, 0)),
            mats,
            mats,
        ],
        out_specs=(whole, whole),
        scratch_shapes=[pltpu.VMEM((RANK, WIDE), F32)],
        compiler_params=pltpu.CompilerParams(vmem_limit_bytes=16 * 2**20),
        cost_estimate=pl.CostEstimate(
            flops=10**6, bytes_accessed=10**5, transcendentals=0
        ),
    )(left, gain_rows, mats_out, mats_value)


def merge_kernel(ours, theirs, own, to_opposite, to_after, to_before):
    total = ours[...] + theirs[...].astype(F32)
    gram = total[:8, SENT : SENT + 128] + total[:8, SENT + 128 :]
    grams = split2(gram)
    own[:, pl.ds(0, SENT)] = total[:8, :SENT]
    own[:, pl.ds(SENT, 128)] = gram
    for slot, target in ((1, to_after), (2, to_opposite), (3, to_before)):
        target[:, pl.ds(0, SENT)] = total[8 * slot : 8 * slot + 8, :SENT].astype(BF16)
        for part, value in enumerate(grams):
            target[:, pl.ds(SENT + 128 * part, 128)] = value


def merge(ours, theirs):
    return pl.pallas_call(
        merge_kernel,
        name="merge",
        out_shape=(
            jax.ShapeDtypeStruct((8, SENT + 128), F32),
            *[jax.ShapeDtypeStruct((8, WIDE), BF16) for _ in range(3)],
        ),
        compiler_params=pltpu.CompilerParams(vmem_limit_bytes=8 * 2**20),
        cost_estimate=pl.CostEstimate(
            flops=10**5, bytes_accessed=7 * 10**5, transcendentals=0
        ),
    )(ours, theirs)


def collect_kernel(own, opposite, after, before, chunk, gram):
    parts = [part[...].astype(F32) for part in (opposite, after, before)]
    total = (own[:, pl.ds(0, SENT)] + parts[0][:, :SENT]) + (
        parts[1][:, :SENT] + parts[2][:, :SENT]
    )
    chunk[...] = total.astype(BF16)
    parts = [part[:, SENT : SENT + 128] + part[:, SENT + 128 :] for part in parts]
    packed = (own[:, pl.ds(SENT, 128)] + parts[0]) + (parts[1] + parts[2])
    square = jnp.concatenate([packed[:, k * RANK : (k + 1) * RANK] for k in range(4)], axis=0)
    wide = jnp.concatenate([square, jnp.zeros((RANK, 128 - RANK), F32)], axis=1)
    for part, value in enumerate(split2(wide)):
        gram[:, pl.ds(part * 128, 128)] = value


def collect(own, opposite, after, before):
    return pl.pallas_call(
        collect_kernel,
        name="collect",
        out_shape=(
            jax.ShapeDtypeStruct((8, SENT), BF16),
            jax.ShapeDtypeStruct((RANK, 256), BF16),
        ),
        compiler_params=pltpu.CompilerParams(vmem_limit_bytes=8 * 2**20),
        cost_estimate=pl.CostEstimate(
            flops=10**5, bytes_accessed=3 * 10**5, transcendentals=0
        ),
    )(own, opposite, after, before)


def factor_kernel(parts, inverse):
    gram = parts[:, pl.ds(0, 128)].astype(F32) + parts[:, pl.ds(128, 128)].astype(F32)
    row_ids = lax.broadcasted_iota(jnp.int32, (RANK, 128), 0)
    col_ids = lax.broadcasted_iota(jnp.int32, (RANK, 128), 1)
    unit = jnp.where(row_ids + RANK == col_ids, 1.0, 0.0)
    work = unit + gram
    for step in range(0, RANK, 2):
        first, second = work[step : step + 1, :], work[step + 1 : step + 2, :]
        column = jnp.broadcast_to(work[:, step : step + 1], (RANK, 128))
        other = jnp.broadcast_to(work[:, step + 1 : step + 2], (RANK, 128))
        scale = 1.0 / column[step : step + 1, :]
        ratio = other[step : step + 1, :] * scale
        other = other - column * ratio
        second = second - first * ratio
        after = row_ids > step + 1
        work = jnp.where(row_ids == step + 1, second, work) - jnp.where(
            after,
            column * (first * scale) + other * (second / other[step + 1 : step + 2, :]),
            0.0,
        )
    diagonal = jnp.sum(jnp.where(row_ids == col_ids, work, 0.0), axis=1, keepdims=True)
    scaled = work * lax.rsqrt(diagonal)
    high, low = split2(pltpu.roll(scaled, 128 - RANK, 1))
    inverse[:, pl.ds(0, 128)] = high
    inverse[:, pl.ds(128, 128)] = low


def factor(parts):
    return pl.pallas_call(
        factor_kernel,
        name="factor",
        out_shape=jax.ShapeDtypeStruct((RANK, 256), BF16),
        cost_estimate=pl.CostEstimate(
            flops=5 * 10**6, bytes_accessed=3 * 10**6, transcendentals=0
        ),
    )(parts)


def finish_kernel(
    ours, theirs, left, mats_out, mats_value,
    err_out, err_value, share_out, share_value, ortho_out, ortho_value, gain_out,
    sums, ortho_parts, right, err_v, sems,
):
    chip, core = place()
    for side, source in ((core, ours), (1 - core, theirs)):
        wide = source[...].astype(F32)
        for block in range(4):
            offset = lax.rem(chip + block, 4) * 8
            rows = pl.ds(pl.multiple_of(side * RANK + offset, 8), 8)
            sums[rows, pl.ds(0, SENT)] = wide[block * 8 : block * 8 + 8, :SENT]
        rows = pl.ds(pl.multiple_of(side * RANK, RANK), RANK)
        sums[rows, pl.ds(SENT, 128)] = wide[:, SENT : SENT + 128] + wide[:, SENT + 128 :]
    copies = []
    for side, (mats, err, scaled) in enumerate(
        ((mats_out, err_out, ortho_out), (mats_value, err_value, ortho_value))
    ):
        span = pl.ds(side * RANK, RANK)
        inverse = sums[span, pl.ds(SENT, 128)][:, :RANK]
        ortho = dot_split(inverse, left[span, :])
        scaled[...] = ortho * math.sqrt(HH)
        high, low = split2(ortho)
        parts = jnp.concatenate([high, low, high, jnp.zeros_like(high)], axis=0)
        ortho_parts[side] = parts.T
        for step in range(STEPS):
            lanes = pl.ds(step * TILE, TILE)
            rows = dot_split(inverse, sums[span, lanes]) * (1.0 / WORKERS)
            right[span, lanes] = rows
            high, low = split2(rows)
            parts = jnp.concatenate([high, high, low, jnp.zeros_like(high)], axis=0)
            err_v[side, :, lanes] = mats[:, lanes].astype(F32) - dot(ortho_parts[side], parts)
            copy = pltpu.make_async_copy(
                err_v.at[side, :, lanes], err.at[0, :, lanes], sems.at[side * STEPS + step]
            )
            copy.start()
            copies.append(copy)
    for part in range(D // 128):
        row = sums[pl.ds(part // 3 * 8 + part % 3, 1), pl.ds(D, 128)]
        gain_out[pl.ds(part * 128, 128)] = row.reshape(128)
    index = chip * 2 + core
    window = right[:, pl.ds(pl.multiple_of(index * 5 // 2 * 128, 128), 512)]
    window = jnp.where(lax.rem(index, 2) == 1, pltpu.roll(window, 512 - 64, 1), window)
    share_out[...] = window[:RANK, : D // 8]
    share_value[...] = window[RANK:, : D // 8]
    for copy in copies:
        copy.wait()


def finish(ours, theirs, left, mats_out, mats_value):
    vmem = pl.BlockSpec(memory_space=pltpu.VMEM)
    return pl.pallas_call(
        finish_kernel,
        name="finish",
        out_shape=(
            jax.ShapeDtypeStruct((1, COLS, D), F32),
            jax.ShapeDtypeStruct((1, COLS, D), F32),
            jax.ShapeDtypeStruct((RANK, D // 8), F32),
            jax.ShapeDtypeStruct((RANK, D // 8), F32),
            jax.ShapeDtypeStruct((RANK, COLS), F32),
            jax.ShapeDtypeStruct((RANK, COLS), F32),
            jax.ShapeDtypeStruct((D,), F32),
        ),
        in_specs=[vmem] * 5,
        out_specs=(ANY, ANY, vmem, vmem, vmem, vmem, vmem),
        scratch_shapes=[
            pltpu.VMEM((2 * RANK, WIDE), F32),
            pltpu.VMEM((2, COLS, 4 * RANK), BF16),
            pltpu.VMEM((2 * RANK, WIDE), F32),
            pltpu.VMEM((2, COLS, D), F32),
            pltpu.SemaphoreType.DMA((2 * STEPS,)),
        ],
        compiler_params=pltpu.CompilerParams(vmem_limit_bytes=24 * 2**20),
        cost_estimate=pl.CostEstimate(
            flops=1 * 10**9, bytes_accessed=13 * 10**6, transcendentals=0
        ),
    )(ours, theirs, left, mats_out, mats_value)


def to_core(value):
    return lax.ppermute(value, "tensor", [(i, i ^ 1) for i in range(8)])


def to_x(value, hops):
    return lax.ppermute(value, "tensor", [(i, (i // 2 + hops) % 4 * 2 + i % 2) for i in range(8)])


def to_z(value, hops):
    return lax.ppermute(value, "dp", [(i, i // 4 * 4 + (i + hops) % 4) for i in range(16)])


def to_y(value, hops):
    return lax.ppermute(value, "dp", [(i, (i // 4 + hops) % 4 * 4 + i % 4) for i in range(16)])


def rounded(value):
    return lax.reduce_precision(value, 8, 7).astype(BF16)


def ring_sum(value, send, beside=()):
    parts = send(value, 2), send(value, 1), send(value, 3)
    parts, beside = lax.optimization_barrier((parts, beside))
    opposite, after, before = (part.astype(F32) for part in parts)
    total = (value.astype(F32) + opposite) + (after + before)
    return (total, *beside) if beside else total


def local(
    hidden_in, ln_gain, attn_probs, w_value, w_out, out_grad, err_out, err_value, factor_codes
):
    w_other = to_core(w_value)
    (
        mats_out, mats_value, left_term, own_half, other_half, gain_rows, hidden_rows, gain_row
    ) = front(
        factor_codes, ln_gain, hidden_in, attn_probs, w_value, w_out, out_grad,
        err_out, err_value,
    )
    received_half = to_core(other_half)

    here, after, before, far_after, far_before = branch(own_half, received_half, w_value, w_other)
    left, far_after, far_before = ring_sum(left_term, to_z, (far_after, far_before))
    far_after, far_before = to_x(far_after, 1), to_x(far_before, 3)
    left = ring_sum(rounded(left), to_y)

    ours, theirs = right_terms(left, gain_rows, mats_out, mats_value)
    theirs, far_after, far_before = lax.optimization_barrier(
        (to_core(theirs), far_after, far_before)
    )
    own, to_opposite, to_after, to_before = merge(ours, theirs)
    next_after, next_before = relay(after, before, far_after, far_before)
    parts = to_x(to_opposite, 2), to_x(to_after, 1), to_x(to_before, 3)
    parts, next_after, next_before = lax.optimization_barrier((parts, next_after, next_before))
    chunk, gram = collect(own, *parts)
    chunk, gram, next_after, next_before = lax.optimization_barrier(
        (chunk, gram, next_after, next_before)
    )
    near_after, near_before = to_x(next_after, 1), to_x(next_before, 3)

    def over_workers(step, carry):
        chunk, inverse = ring_sum(carry[0], to_z, (factor(carry[1]),))
        return rounded(ring_sum(rounded(chunk), to_y)), inverse

    passes = 1 + lax.axis_index("dp") // WORKERS
    chunk, inverse = lax.fori_loop(0, passes, over_workers, (chunk, gram))
    chunk, near_after, near_before = lax.optimization_barrier((chunk, near_after, near_before))
    in_grad = norm_back(hidden_rows, gain_row, here, near_after, near_before)
    parts = to_x(chunk, 2), to_x(chunk, 3), to_x(chunk, 1)
    (opposite, after, before), in_grad = lax.optimization_barrier((parts, in_grad))
    rows = jnp.concatenate([chunk, after, opposite, before], axis=0)
    ours = jnp.concatenate([rows, inverse], axis=1)
    theirs = to_core(ours)
    new_out, new_value, share_out, share_value, ortho_out, ortho_value, gain_grad = finish(
        ours, theirs, left, mats_out, mats_value
    )
    return (
        in_grad,
        gain_grad,
        new_out,
        new_value,
        ortho_out.T,
        ortho_value.T,
        share_out.T,
        share_value.T,
    )


def solution(mesh):
    in_specs = (
        P("dp", None),
        P(),
        P("dp", "tensor", None, None),
        P(None, "tensor"),
        P("tensor", None),
        P("dp", None),
        P("dp", "tensor", None),
        P("dp", "tensor", None),
        P(),
    )
    out_specs = (
        P(("dp", "tensor"), None),
        P(),
        P("dp", "tensor", None),
        P("dp", "tensor", None),
        P("tensor", None),
        P("tensor", None),
        P("tensor", None),
        P("tensor", None),
    )
    return jax.shard_map(local, mesh=mesh, in_specs=in_specs, out_specs=out_specs, check_vma=False)
```
